32 devices in a mesh: hour: 4 (over y, core), lat: 2 (over x), lon: 4 (over z).
Axes of the slice: x: 2, y: 2, z: 4, core: 2. Of those that a mesh axis runs over, the one named last changes fastest.
Arguments:
- precip: float32 [4, 1024, 2048], P('hour', 'lat', 'lon'), may hold values from 0.05 to 5
- scaling: float32 [4, 1024, 2048], P('hour', 'lat', 'lon'), may hold values from 0.5 to 2
- hour_weight: float32 [4], P('hour'), may hold values from 0.03 to 0.3
- cotangent: float32 [4, 1024, 2048], P('hour', 'lat', 'lon'), may hold values from -6 to 6
Outputs:
- grad_precip: float32 [4, 1024, 2048], P('hour', 'lat', 'lon')
- grad_scaling: float32 [4, 1024, 2048], P('hour', 'lat', 'lon')
The draws below stay inside these ranges and needn't reach their ends.
All inputs are finite; a program needn't handle non-finite values.
Results may differ from the reference program's by a relative error of at most 0.00012.
Values sent between devices are 32-bit elements; how exact they have to be, the bound alone decides.
A program may use at most 64 MiB of HBM per device.

```python
import math
import jax
import jax.numpy as jnp
from jax import lax

RADIUS = 8
HOURS = 4
NLAT = 1024
NLON = 2048


def steps_of(own_key, dims, shards, low, high):
    def one(axis_at, parts):
        steps = jax.random.uniform(jax.random.fold_in(jax.random.fold_in(own_key, 6), axis_at), (parts,), jnp.float32, low / len(shards), high / len(shards))
        return jnp.repeat(jnp.exp(steps), dims[axis_at] // parts).reshape((-1,) + (1,) * (len(dims) - axis_at - 1))

    level = one(*shards[0])
    for cut in shards[1:]:
        level = level * one(*cut)
    return level


def noise(rng, extent, spread, bound, pieces=(), dtype=jnp.bfloat16):
    entries = jax.random.normal(rng, extent, jnp.float32) * spread
    if len(pieces) > 0:
        entries = steps_of(rng, extent, pieces, -0.22, 0.18) * entries
    return jnp.clip(entries, min=-bound, max=bound).astype(dtype)


def setup_inputs(seed: int = 0) -> dict:
    key_list = jax.random.split(jax.random.key(seed), 5)
    precip = jnp.clip(jnp.exp(math.log(5.0) - 4.6051702 * jax.random.uniform(key_list[0], (HOURS, NLAT, NLON), jnp.float32) ** steps_of(key_list[0], (HOURS, NLAT, NLON), ((0, 4), (1, 2), (2, 4)), -0.2, 0.2)), 0.05, 5.0)
    scaling = jnp.clip(jnp.exp(math.log(2.0) - 1.3862944 * jax.random.uniform(key_list[1], (HOURS, NLAT, NLON), jnp.float32) ** steps_of(key_list[1], (HOURS, NLAT, NLON), ((0, 4), (1, 2), (2, 4)), -0.2, 0.2)), 0.5, 2.0)
    hour_weight = jnp.clip(jnp.exp(math.log(0.3) - 2.3025852 * jax.random.uniform(key_list[2], (HOURS,), jnp.float32) ** steps_of(key_list[2], (HOURS,), ((0, 4),), -0.2, 0.2)), 0.03, 0.3)
    cotangent = noise(key_list[3], (HOURS, NLAT, NLON), 1.0, 6.0, ((0, 4), (1, 2), (2, 4)), jnp.float32)
    return dict(precip=precip, scaling=scaling, hour_weight=hour_weight, cotangent=cotangent)


PHI = 0.8
SPREAD = 50.0


def kernel_taps():
    offsets = jnp.arange(-RADIUS, RADIUS + 1).astype(jnp.float32)
    values = jnp.exp(-offsets * offsets / SPREAD)
    return values / jnp.sum(values)


def smooth(field):
    taps = kernel_taps()
    rows = field.shape[0]
    padded = jnp.pad(field, ((RADIUS, RADIUS), (0, 0)))
    across = taps[0] * padded[0:rows]
    for step in range(1, 2 * RADIUS + 1):
        across = across + taps[step] * padded[step:step + rows]
    result = taps[0] * jnp.roll(across, RADIUS, axis=1)
    for step in range(1, 2 * RADIUS + 1):
        result = result + taps[step] * jnp.roll(across, RADIUS - step, axis=1)
    return result


def forward_hour(precip_hour, scaling_hour):
    first = smooth(scaling_hour)
    lifted = jnp.power(precip_hour / first, PHI)
    second = smooth(lifted)
    return first, lifted, second


def reference(precip, scaling, hour_weight, cotangent):
    def log_part(pair):
        return jnp.log(forward_hour(pair[0], pair[1])[2])

    logb = lax.map(log_part, (precip, scaling))
    logq = jnp.sum(hour_weight[:, None, None] * logb, axis=0)
    terms = PHI * cotangent * jnp.exp(PHI * (logq[None] - logb))
    dlogq = jnp.sum(terms, axis=0)

    def back_hour(items):
        precip_hour, scaling_hour, term, weight = items
        first, lifted, second = forward_hour(precip_hour, scaling_hour)
        dsecond = (weight * dlogq - term) / second
        dlifted = smooth(dsecond)
        carried = PHI * dlifted * lifted
        return carried / precip_hour, smooth(-carried / first)

    grad_precip, grad_scaling = lax.map(back_hour, (precip, scaling, terms, hour_weight))
    return grad_precip, grad_scaling
```

```python
import functools
import math
import jax
import jax.numpy as jnp
from jax import lax
from jax.experimental import pallas as pl
from jax.experimental.pallas import tpu as pltpu
from jax.sharding import PartitionSpec as P

RADIUS = 8
PHI = 0.8
SPREAD = 50.0
STEP = 128
EDGE = 2 * RADIUS
TOTAL = sum(math.exp(-d * d / SPREAD) for d in range(-RADIUS, RADIUS + 1))
MESH = pl.DeviceIdType.MESH
F32, BF16 = jnp.float32, jnp.bfloat16
TALL = STEP + 3 * EDGE


def split(x):
    high = x.astype(BF16)
    return high, (x - high.astype(F32)).astype(BF16)


def band(rows, cols, shift):
    i = lax.broadcasted_iota(jnp.int32, (rows, cols), 0)
    j = lax.broadcasted_iota(jnp.int32, (rows, cols), 1)
    d = (j - i - shift).astype(F32)
    return jnp.where(jnp.abs(d) <= RADIUS, jnp.exp(-d * d / SPREAD) / TOTAL, 0.0)


def dot(a, b):
    return jnp.dot(a, b, preferred_element_type=F32)


def kernel(
    sizes, p_hbm, s_hbm, w_ref, c_hbm, gp_hbm, gs_hbm,
    es, ep, ct, first, lift, ds, own, got, part, other, both, scale,
    st_l, st_r, h_l, h_r, sd_l, sd_r, hd_l, hd_r, o_p, o_s,
    t_hi, t_lo, b_hi, b_lo, local, sends, recvs,
):
    n_hour, n_lat, n_lon, rows, cols = sizes
    chunks = rows // STEP
    tall, wide = rows + 2 * EDGE, cols + STEP
    bits = n_hour.bit_length() - 1
    hour, lat, lon = (lax.axis_index(a) for a in ("hour", "lat", "lon"))
    side = lax.rem(hour, 2)
    up, down = lax.rem(lat + n_lat - 1, n_lat), lax.rem(lat + 1, n_lat)
    left, right = lax.rem(lon + n_lon - 1, n_lon), lax.rem(lon + 1, n_lon)

    def flip(bit):
        m = 1 << bit
        return hour + m - 2 * m * lax.rem(hour // m, 2)

    loads = [
        pltpu.make_async_copy(s_hbm.at[0], es.at[pl.ds(EDGE, rows), pl.ds(0, cols)], local.at[0]),
        pltpu.make_async_copy(p_hbm.at[0], ep.at[pl.ds(EDGE, rows), pl.ds(0, cols)], local.at[1]),
        pltpu.make_async_copy(c_hbm.at[0], ct, local.at[2]),
    ]
    for copy in loads:
        copy.start()

    barrier = pltpu.get_barrier_semaphore()
    lats = [up, down] if n_lat > 2 else [down]
    lons = [left, right] if n_lon > 2 else [right]
    peers = [{"lon": z} for z in lons] + [{"lat": x} for x in lats]
    peers += [{"lat": x, "lon": z} for x in lats for z in lons]
    peers += [{"hour": flip(bit)} for bit in range(bits)]
    for peer in peers:
        pl.semaphore_signal(barrier, inc=1, device_id=peer, device_id_type=MESH)

    hi, lo = split(band(t_hi.shape[0], t_hi.shape[1], -STEP).astype(F32))
    t_hi[...], t_lo[...] = hi, lo
    hi, lo = split(band(b_hi.shape[0], b_hi.shape[1], RADIUS))
    b_hi[...], b_lo[...] = hi, lo

    pl.semaphore_wait(barrier, len(peers))

    sent = []

    def send(src, dst, peer):
        at = len(sent)
        copy = pltpu.make_async_remote_copy(
            src_ref=src, dst_ref=dst, send_sem=sends.at[at], recv_sem=recvs.at[at],
            device_id=peer, device_id_type=MESH,
        )
        copy.start()
        sent.append(copy)
        return copy

    def row_pass(x, n):
        xh, xl = split(x)
        bh, bl = b_hi[0:n, 0 : n + EDGE], b_lo[0:n, 0 : n + EDGE]
        return dot(bh, xh) + (dot(bh, xl) + dot(bl, xh))

    def col_pass(x, width):
        xh, xl = split(x)
        blocks = wide // STEP
        out = []
        for start in range(0, width, 2 * STEP):
            size = min(2 * STEP, width - start)
            picks = [(start // STEP - 1 + i) % blocks for i in range(size // STEP + 2)]
            a = jnp.concatenate([xh[:, i * STEP : (i + 1) * STEP] for i in picks], axis=1)
            b = jnp.concatenate([xl[:, i * STEP : (i + 1) * STEP] for i in picks], axis=1)
            depth = size + 2 * STEP
            th, tl = t_hi[0:depth, 0:size], t_lo[0:depth, 0:size]
            out.append(dot(a, th) + (dot(b, th) + dot(a, tl)))
        return jnp.concatenate(out, axis=1)

    arrive = []
    for src, dst in ((s_hbm, es), (p_hbm, ep)):
        arrive.append(send(src.at[0, pl.ds(0, EDGE)], dst.at[pl.ds(EDGE + rows, EDGE), pl.ds(0, cols)], {"lat": up}))
        arrive.append(send(src.at[0, pl.ds(rows - EDGE, EDGE)], dst.at[pl.ds(0, EDGE), pl.ds(0, cols)], {"lat": down}))
    loads[0].wait()
    own_rows = pl.ds(EDGE, rows)
    st_l[0:EDGE, :] = es[own_rows, 0:STEP].T[0:EDGE]
    st_r[0:EDGE, :] = es[own_rows, cols - STEP : cols].T[STEP - EDGE :]
    loads[1].wait()
    st_l[EDGE : EDGE + RADIUS, :] = ep[own_rows, 0:STEP].T[0:RADIUS]
    st_r[EDGE : EDGE + RADIUS, :] = ep[own_rows, cols - STEP : cols].T[STEP - RADIUS :]
    first_lanes, last_lanes = pl.ds(0, STEP), pl.ds(rows - STEP, STEP)
    for stage, dst, z in ((st_l, h_r, left), (st_r, h_l, right)):
        arrive.append(send(stage, dst.at[:, pl.ds(STEP, rows)], {"lon": z}))
        arrive.append(send(stage.at[:, first_lanes], dst.at[:, pl.ds(STEP + rows, STEP)], {"lat": up, "lon": z}))
        arrive.append(send(stage.at[:, last_lanes], dst.at[:, pl.ds(0, STEP)], {"lat": down, "lon": z}))
    for copy in arrive:
        copy.wait_recv()
    lanes = rows + 2 * STEP
    ones = jnp.ones((STEP - 2 * EDGE, lanes), F32)
    block = jnp.concatenate([h_r[0:EDGE], ones, h_l[0:EDGE]], axis=0).T
    es[:, cols:wide] = block[STEP - EDGE : STEP + rows + EDGE]
    ones = jnp.ones((STEP - 2 * RADIUS, lanes), F32)
    block = jnp.concatenate([h_r[EDGE:], ones, h_l[EDGE:]], axis=0).T
    ep[:, cols:wide] = block[STEP - EDGE : STEP + rows + EDGE]
    top, bottom = slice(0, EDGE), slice(EDGE + rows, tall)
    es[top, :] = jnp.where(lat > 0, es[top, :], 0.0)
    es[bottom, :] = jnp.where(lat < n_lat - 1, es[bottom, :], 0.0)
    loads[2].wait()
    weight = w_ref[0]

    def forward(c):
        at = c * STEP
        span = slice(at + RADIUS, at + RADIUS + STEP + EDGE)
        a = col_pass(row_pass(es[at : at + STEP + 2 * EDGE, :], STEP + EDGE), wide)
        first[span, :] = a
        u = jnp.exp(PHI * jnp.log(ep[span, :] / a))
        if c == 0 or c == chunks - 1:
            e = lax.broadcasted_iota(jnp.int32, u.shape, 0) + (at + RADIUS)
            inside = ((lat > 0) | (e >= EDGE)) & ((lat < n_lat - 1) | (e < EDGE + rows))
            u = jnp.where(inside, u, 0.0)
        lift[span, :] = u
        b = col_pass(row_pass(u, STEP), cols)
        logb = jnp.log(b)
        mine = slice(at, at + STEP)
        own[0, mine, :] = weight * logb
        own[1, mine, :] = ct[mine, :] * jnp.exp(-PHI * logb)
        scale[mine, :] = PHI / b
        r = pl.ds(at, STEP)
        return send(own.at[1 - side, r], got.at[r], {"hour": flip(0)})

    def join(c, bit, copy):
        copy.wait_recv()
        at = c * STEP
        mine = slice(at, at + STEP)
        r = pl.ds(at, STEP)
        if bit == 0:
            value = own[side, mine, :] + got[mine, :]
        else:
            value = part[bit - 1, mine, :] + other[bit - 1, mine, :]
        if bit == bits - 1:
            both[side, mine, :] = value
            return send(both.at[side, r], both.at[side, r], {"hour": flip(0)})
        part[bit, mine, :] = value
        return send(part.at[bit, r], other.at[bit, r], {"hour": flip(bit + 1)})

    def second(c, copy):
        copy.wait_recv()
        at = c * STEP
        mine = slice(at, at + STEP)
        d = jnp.exp(PHI * both[0, mine, :]) * (weight * both[1, mine, :] - own[1, mine, :]) * scale[mine, :]
        ds[at + EDGE : at + EDGE + STEP, 0:cols] = d
        sd_l[:, mine] = d[:, 0:STEP].T[0:EDGE]
        sd_r[:, mine] = d[:, cols - STEP : cols].T[STEP - EDGE :]
        r = pl.ds(at, STEP)
        main, corner = [], []
        if c == 0:
            corner.append(send(ds.at[pl.ds(EDGE, EDGE), pl.ds(0, cols)], ds.at[pl.ds(EDGE + rows, EDGE), pl.ds(0, cols)], {"lat": up}))
        if c == chunks - 1:
            corner.append(send(ds.at[pl.ds(rows, EDGE), pl.ds(0, cols)], ds.at[pl.ds(0, EDGE), pl.ds(0, cols)], {"lat": down}))
        for stage, dst, z in ((sd_l, hd_r, left), (sd_r, hd_l, right)):
            main.append(send(stage.at[:, r], dst.at[:, pl.ds(STEP + at, STEP)], {"lon": z}))
            if c == 0:
                corner.append(send(stage.at[:, r], dst.at[:, pl.ds(STEP + rows, STEP)], {"lat": up, "lon": z}))
            if c == chunks - 1:
                corner.append(send(stage.at[:, r], dst.at[:, pl.ds(0, STEP)], {"lat": down, "lon": z}))
        return main, corner

    def side_block(i):
        zeros = jnp.zeros((STEP - 2 * EDGE, STEP), F32)
        at = slice(i * STEP, (i + 1) * STEP)
        return jnp.concatenate([hd_r[:, at], zeros, hd_l[:, at]], axis=0).T

    def take_main(c, copies):
        for copy in copies:
            copy.wait_recv()
        ds[EDGE + c * STEP : EDGE + (c + 1) * STEP, cols:wide] = side_block(c + 1)

    def take_corners(copies):
        for copy in copies:
            copy.wait_recv()
        ds[top, cols:wide] = side_block(0)[STEP - EDGE :]
        ds[bottom, cols:wide] = side_block(chunks + 1)[0:EDGE]
        ds[top, :] = jnp.where(lat > 0, ds[top, :], 0.0)
        ds[bottom, :] = jnp.where(lat < n_lat - 1, ds[bottom, :], 0.0)

    stores = []

    def backward(at, n):
        span = slice(at + RADIUS, at + n + 3 * RADIUS)
        d = col_pass(row_pass(ds[at : at + n + 2 * EDGE, :], n + EDGE), wide)
        carried = PHI * d * lift[span, :]
        mine = slice(at, at + n)
        o_p[mine, :] = carried[RADIUS : RADIUS + n, 0:cols] / ep[at + EDGE : at + EDGE + n, 0:cols]
        o_s[mine, :] = col_pass(row_pass(-carried / first[span, :], n), cols)
        r = pl.ds(at, n)
        for src, dst in ((o_p, gp_hbm), (o_s, gs_hbm)):
            copy = pltpu.make_async_copy(src.at[r], dst.at[0, r], local.at[3 + len(stores)])
            copy.start()
            stores.append(copy)

    order = [0, chunks - 1] + list(range(1, chunks - 1))
    moving = {}
    waiting = None
    for c in order:
        moving[c] = forward(c)
        if waiting is not None:
            moving[waiting] = join(waiting, 0, moving[waiting])
        waiting = c
    moving[waiting] = join(waiting, 0, moving[waiting])
    for bit in range(1, bits - 1):
        for c in order:
            moving[c] = join(c, bit, moving[c])
    mains, corners = {}, []
    done = 0
    for c in order:
        if bits > 1:
            moving[c] = join(c, bits - 1, moving[c])
        mains[c], corner = second(c, moving[c])
        corners += corner
        if c not in (0, chunks - 1):
            if done == 0:
                take_main(0, mains[0])
                take_main(chunks - 1, mains[chunks - 1])
                take_corners(corners)
                backward((chunks - 1) * STEP + EDGE, STEP - EDGE)
                backward(0, STEP - EDGE)
                done = STEP - EDGE
            take_main(c, mains[c])
            end = (c + 1) * STEP + (EDGE if c == chunks - 2 else -EDGE)
            backward(done, end - done)
            done = end
    for copy in sent:
        copy.wait_send()
    for copy in stores:
        copy.wait()


def per_device(n_hour, n_lat, n_lon, precip, scaling, hour_weight, cotangent):
    rows, cols = precip.shape[1:]
    tall, wide, lanes = rows + 2 * EDGE, cols + STEP, rows + 2 * STEP
    bits = n_hour.bit_length() - 1
    chunks = rows // STEP
    assert n_hour == 1 << bits and bits > 0 and min(n_lat, n_lon) > 1
    assert rows % STEP == 0 and cols % (2 * STEP) == 0 and chunks > 2
    ext, tile = pltpu.VMEM((tall, wide), F32), pltpu.VMEM((rows, cols), F32)
    pair = pltpu.VMEM((2, rows, cols), F32)
    steps = pltpu.VMEM((max(bits - 1, 1), rows, cols), F32)
    copies = 10 + chunks * (bits + 3) + 6
    out = jax.ShapeDtypeStruct(precip.shape, F32)
    hbm = pl.BlockSpec(memory_space=pl.ANY)
    return pl.pallas_call(
        functools.partial(kernel, (n_hour, n_lat, n_lon, rows, cols)),
        out_shape=(out, out),
        in_specs=[hbm, hbm, pl.BlockSpec(memory_space=pltpu.SMEM), hbm],
        out_specs=(hbm, hbm),
        scratch_shapes=[
            ext, ext, tile, ext, ext, ext, pair, tile, steps, steps, pair, tile,
            pltpu.VMEM((EDGE + RADIUS, rows), F32), pltpu.VMEM((EDGE + RADIUS, rows), F32),
            pltpu.VMEM((EDGE + RADIUS, lanes), F32), pltpu.VMEM((EDGE + RADIUS, lanes), F32),
            pltpu.VMEM((EDGE, rows), F32), pltpu.VMEM((EDGE, rows), F32),
            pltpu.VMEM((EDGE, lanes), F32), pltpu.VMEM((EDGE, lanes), F32),
            tile, tile,
            pltpu.VMEM((4 * STEP, 2 * STEP), BF16), pltpu.VMEM((4 * STEP, 2 * STEP), BF16),
            pltpu.VMEM((TALL, TALL + EDGE), BF16), pltpu.VMEM((TALL, TALL + EDGE), BF16),
            pltpu.SemaphoreType.DMA((3 + 2 * (chunks + 1),)),
            pltpu.SemaphoreType.DMA((copies,)), pltpu.SemaphoreType.DMA((copies,)),
        ],
        compiler_params=pltpu.CompilerParams(
            collective_id=0, has_side_effects=True, vmem_limit_bytes=56 * 1024 * 1024
        ),
    )(precip, scaling, hour_weight, cotangent)


def solution(mesh):
    field = P("hour", "lat", "lon")
    sizes = [mesh.shape[a] for a in ("hour", "lat", "lon")]
    return jax.shard_map(
        functools.partial(per_device, *sizes), mesh=mesh,
        in_specs=(field, field, P("hour"), field), out_specs=(field, field), check_vma=False,
    )
```

```python
import functools
import math
import jax
import jax.numpy as jnp
from jax import lax
from jax.experimental import pallas as pl
from jax.experimental.pallas import tpu as pltpu
from jax.sharding import PartitionSpec as P

RADIUS = 8
PHI = 0.8
SPREAD = 50.0
STEP = 128
EDGE = 2 * RADIUS
TOTAL = sum(math.exp(-d * d / SPREAD) for d in range(-RADIUS, RADIUS + 1))
MESH = pl.DeviceIdType.MESH
F32, BF16 = jnp.float32, jnp.bfloat16


def split(x):
    high = x.astype(BF16)
    return high, (x - high.astype(F32)).astype(BF16)


def band(rows, cols, shift):
    i = lax.broadcasted_iota(jnp.int32, (rows, cols), 0)
    j = lax.broadcasted_iota(jnp.int32, (rows, cols), 1)
    d = (j - i - shift).astype(F32)
    return jnp.where(jnp.abs(d) <= RADIUS, jnp.exp(-d * d / SPREAD) / TOTAL, 0.0)


def stacked_rows(n):
    j = lax.broadcasted_iota(jnp.int32, (n, 3 * (n + EDGE)), 1)
    parts = []
    for at in range(3):
        full = band(n, 3 * (n + EDGE), RADIUS + at * (n + EDGE))
        high = full.astype(BF16).astype(F32)
        parts.append(full - high if at == 2 else high)
    depth = n + EDGE
    return jnp.where(j < depth, parts[0], jnp.where(j < 2 * depth, parts[1], parts[2])).astype(BF16)


def stacked_cols(size):
    own_high, own_low = split(band(size, size, 0))
    i = lax.broadcasted_iota(jnp.int32, (STEP, size), 0)
    j = lax.broadcasted_iota(jnp.int32, (STEP, size), 1)

    def beside(lane):
        d = (jnp.where(lane >= STEP // 2, lane - STEP, lane + size) - j).astype(F32)
        return jnp.where(jnp.abs(d) <= RADIUS, jnp.exp(-d * d / SPREAD) / TOTAL, 0.0)

    first = beside(i).astype(BF16)
    middle = (i >= STEP // 4) & (i < 3 * STEP // 4)
    moved = beside(jnp.where(i < STEP // 2, i + STEP // 2, i - STEP // 2))
    low = moved - moved.astype(BF16).astype(F32)
    second = jnp.where(middle, low, first.astype(F32)).astype(BF16)
    return jnp.concatenate([own_high, own_high, own_low, first, second], axis=0)


def plan(rows):
    sizes = [STEP // 2] + [STEP] * ((rows - 2 * STEP) // STEP) + [STEP // 2, STEP]
    pieces = [(sum(sizes[:i]), n) for i, n in enumerate(sizes)]
    last = len(pieces) - 1
    return pieces, [0, last] + list(range(1, last))


def heights(rows):
    found = set()
    pieces, _ = plan(rows)
    for _, n in pieces:
        found |= {n, n + EDGE}
    for _, n in regions(rows):
        found |= {n, n + EDGE}
    return sorted(found)


def regions(rows):
    pieces, order = plan(rows)
    last = len(pieces) - 1
    found = [(0, pieces[0][1] - EDGE), (pieces[last][0] + EDGE, pieces[last][1] - EDGE)]
    at = found[0][1]
    for c in order[2:]:
        end = sum(pieces[c]) + (EDGE if c == last - 1 else -EDGE)
        found.append((at, end - at))
        at = end
    return found


def kernel(
    sizes, p_hbm, s_hbm, w_ref, c_hbm, o_p, o_s,
    es, ep, ct, first, lift, ds, own, got, part, other, both, scale,
    st_l, st_r, h_l, h_r, sd_l, sd_r, hd_l, hd_r, t_pair, t_last,
    local, sends, recvs, *bands,
):
    n_hour, n_lat, n_lon, rows, cols = sizes
    pieces, order = plan(rows)
    count = len(pieces)
    by_height = dict(zip(heights(rows), bands))
    tall, wide = rows + 2 * EDGE, cols + STEP
    bits = n_hour.bit_length() - 1
    hour, lat, lon = (lax.axis_index(a) for a in ("hour", "lat", "lon"))
    side = lax.rem(hour, 2)
    up, down = lax.rem(lat + n_lat - 1, n_lat), lax.rem(lat + 1, n_lat)
    left, right = lax.rem(lon + n_lon - 1, n_lon), lax.rem(lon + 1, n_lon)

    def flip(bit):
        m = 1 << bit
        return hour + m - 2 * m * lax.rem(hour // m, 2)

    own_rows = pl.ds(EDGE, rows)
    loads = []
    for z, n in ((0, STEP), (cols - STEP, STEP), (STEP, cols - 2 * STEP)):
        for src, dst in ((s_hbm, es), (p_hbm, ep)):
            lanes = pl.ds(z, n)
            loads.append(pltpu.make_async_copy(src.at[0, :, lanes], dst.at[own_rows, lanes], local.at[len(loads)]))
    loads.append(pltpu.make_async_copy(c_hbm.at[0], ct, local.at[len(loads)]))
    for copy in loads:
        copy.start()

    barrier = pltpu.get_barrier_semaphore()
    lats = [up, down] if n_lat > 2 else [down]
    lons = [left, right] if n_lon > 2 else [right]
    peers = [{"lon": z} for z in lons] + [{"lat": x} for x in lats]
    peers += [{"lat": x, "lon": z} for x in lats for z in lons]
    peers += [{"hour": flip(bit)} for bit in range(bits)]
    for peer in peers:
        pl.semaphore_signal(barrier, inc=1, device_id=peer, device_id_type=MESH)

    t_pair[...] = stacked_cols(2 * STEP)
    t_last[...] = stacked_cols(STEP)
    for n, ref in by_height.items():
        ref[...] = stacked_rows(n)
    sd_l[...] = jnp.zeros_like(sd_l)
    sd_r[...] = jnp.zeros_like(sd_r)

    pl.semaphore_wait(barrier, len(peers))

    sent = []

    def send(src, dst, peer):
        at = len(sent)
        copy = pltpu.make_async_remote_copy(
            src_ref=src, dst_ref=dst, send_sem=sends.at[at], recv_sem=recvs.at[at],
            device_id=peer, device_id_type=MESH,
        )
        copy.start()
        sent.append(copy)
        return copy

    def row_pass(x, n):
        high, low = split(x)
        return jnp.dot(
            by_height[n][...], jnp.concatenate([high, low, high], axis=0), preferred_element_type=F32
        )

    def col_pass(x, width):
        high, low = split(x)
        blocks = wide // STEP
        lane = lax.broadcasted_iota(jnp.int32, (x.shape[0], STEP), 1)
        middle = (lane >= STEP // 4) & (lane < 3 * STEP // 4)
        out = []
        for start in range(0, width, 2 * STEP):
            size = min(2 * STEP, width - start)
            before = (start // STEP - 1) % blocks * STEP
            after = (start + size) // STEP % blocks * STEP
            beside = jnp.where(lane >= STEP // 2, x[:, before : before + STEP], x[:, after : after + STEP])
            near = beside.astype(BF16)
            rounded = near.astype(F32)
            mixed = jnp.where(middle, pltpu.roll(rounded, STEP // 2, 1), beside - rounded).astype(BF16)
            h, l = high[:, start : start + size], low[:, start : start + size]
            weights = t_pair if size == 2 * STEP else t_last
            out.append(jnp.dot(
                jnp.concatenate([h, l, h, near, mixed], axis=1), weights[...], preferred_element_type=F32
            ))
        return jnp.concatenate(out, axis=1)

    arrive = []
    for src, dst in ((s_hbm, es), (p_hbm, ep)):
        arrive.append(send(src.at[0, pl.ds(0, EDGE)], dst.at[pl.ds(EDGE + rows, EDGE), pl.ds(0, cols)], {"lat": up}))
        arrive.append(send(src.at[0, pl.ds(rows - EDGE, EDGE)], dst.at[pl.ds(0, EDGE), pl.ds(0, cols)], {"lat": down}))
    loads[0].wait()
    loads[2].wait()
    st_l[0:EDGE, :] = es[own_rows, 0:STEP].T[0:EDGE]
    st_r[0:EDGE, :] = es[own_rows, cols - STEP : cols].T[STEP - EDGE :]
    loads[1].wait()
    loads[3].wait()
    st_l[EDGE : EDGE + RADIUS, :] = ep[own_rows, 0:STEP].T[0:RADIUS]
    st_r[EDGE : EDGE + RADIUS, :] = ep[own_rows, cols - STEP : cols].T[STEP - RADIUS :]
    first_lanes, last_lanes = pl.ds(0, STEP), pl.ds(rows - STEP, STEP)
    for stage, dst, z in ((st_l, h_r, left), (st_r, h_l, right)):
        arrive.append(send(stage, dst.at[:, pl.ds(STEP, rows)], {"lon": z}))
        arrive.append(send(stage.at[:, first_lanes], dst.at[:, pl.ds(STEP + rows, STEP)], {"lat": up, "lon": z}))
        arrive.append(send(stage.at[:, last_lanes], dst.at[:, pl.ds(0, STEP)], {"lat": down, "lon": z}))
    for copy in loads[4:]:
        copy.wait()
    for copy in arrive:
        copy.wait_recv()
    lanes = rows + 2 * STEP
    ones = jnp.ones((STEP - 2 * EDGE, lanes), F32)
    block = jnp.concatenate([h_r[0:EDGE], ones, h_l[0:EDGE]], axis=0).T
    es[:, cols:wide] = block[STEP - EDGE : STEP + rows + EDGE]
    ones = jnp.ones((STEP - 2 * RADIUS, lanes), F32)
    block = jnp.concatenate([h_r[EDGE:], ones, h_l[EDGE:]], axis=0).T
    ep[:, cols:wide] = block[STEP - EDGE : STEP + rows + EDGE]
    top, bottom = slice(0, EDGE), slice(EDGE + rows, tall)
    es[top, :] = jnp.where(lat > 0, es[top, :], 0.0)
    es[bottom, :] = jnp.where(lat < n_lat - 1, es[bottom, :], 0.0)
    weight = w_ref[0]

    def lifted(c):
        at, n = pieces[c]
        span = slice(at + RADIUS, at + RADIUS + n + EDGE)
        a = col_pass(row_pass(es[at : at + n + 2 * EDGE, :], n + EDGE), wide)
        first[span, :] = a
        u = jnp.exp(PHI * jnp.log(ep[span, :] / a))
        if c == 0 or c == count - 1:
            e = lax.broadcasted_iota(jnp.int32, u.shape, 0) + (at + RADIUS)
            inside = ((lat > 0) | (e >= EDGE)) & ((lat < n_lat - 1) | (e < EDGE + rows))
            u = jnp.where(inside, u, 0.0)
        lift[span, :] = u

    def logs(c):
        at, n = pieces[c]
        b = col_pass(row_pass(lift[at + RADIUS : at + RADIUS + n + EDGE, :], n), cols)
        logb = jnp.log(b)
        mine = slice(at, at + n)
        own[0, mine, :] = weight * logb
        own[1, mine, :] = ct[mine, :] * jnp.exp(-PHI * logb)
        scale[mine, :] = PHI / b
        r = pl.ds(at, n)
        return send(own.at[1 - side, r], got.at[r], {"hour": flip(0)})

    def join(c, bit, copy):
        copy.wait_recv()
        at, n = pieces[c]
        mine = slice(at, at + n)
        r = pl.ds(at, n)
        if bit == 0:
            value = own[side, mine, :] + got[mine, :]
        else:
            value = part[bit - 1, mine, :] + other[bit - 1, mine, :]
        if bit == bits - 1:
            both[side, mine, :] = value
            return send(both.at[side, r], both.at[side, r], {"hour": flip(0)})
        part[bit, mine, :] = value
        return send(part.at[bit, r], other.at[bit, r], {"hour": flip(bit + 1)})

    def second(c, copy):
        copy.wait_recv()
        at, n = pieces[c]
        mine = slice(at, at + n)
        d = jnp.exp(PHI * both[0, mine, :]) * (weight * both[1, mine, :] - own[1, mine, :]) * scale[mine, :]
        ds[at + EDGE : at + EDGE + n, 0:cols] = d
        sd_l[c, :, 0:n] = d[:, 0:STEP].T[0:EDGE]
        sd_r[c, :, 0:n] = d[:, cols - STEP : cols].T[STEP - EDGE :]
        main, corner = [], []
        inner = pl.ds(0, cols)
        if c == 0:
            corner.append(send(ds.at[pl.ds(EDGE, EDGE), inner], ds.at[pl.ds(EDGE + rows, EDGE), inner], {"lat": up}))
        if c == count - 1:
            corner.append(send(ds.at[pl.ds(rows, EDGE), inner], ds.at[pl.ds(0, EDGE), inner], {"lat": down}))
        for stage, dst, z in ((sd_l, hd_r, left), (sd_r, hd_l, right)):
            main.append(send(stage.at[c], dst.at[c + 1], {"lon": z}))
            if c == 0:
                corner.append(send(stage.at[c], dst.at[count + 1], {"lat": up, "lon": z}))
            if c == count - 1:
                corner.append(send(stage.at[c], dst.at[0], {"lat": down, "lon": z}))
        return main, corner

    def side_block(i, n):
        zeros = jnp.zeros((STEP - 2 * EDGE, n), F32)
        return jnp.concatenate([hd_r[i, :, 0:n], zeros, hd_l[i, :, 0:n]], axis=0).T

    def take_main(c, copies):
        for copy in copies:
            copy.wait_recv()
        at, n = pieces[c]
        ds[EDGE + at : EDGE + at + n, cols:wide] = side_block(c + 1, n)

    def take_corners(copies):
        for copy in copies:
            copy.wait_recv()
        n = pieces[count - 1][1]
        ds[top, cols:wide] = side_block(0, n)[n - EDGE :]
        ds[bottom, cols:wide] = side_block(count + 1, pieces[0][1])[0:EDGE]
        ds[top, :] = jnp.where(lat > 0, ds[top, :], 0.0)
        ds[bottom, :] = jnp.where(lat < n_lat - 1, ds[bottom, :], 0.0)

    def backward(at, n):
        span = slice(at + RADIUS, at + n + 3 * RADIUS)
        d = col_pass(row_pass(ds[at : at + n + 2 * EDGE, :], n + EDGE), wide)
        carried = PHI * d * lift[span, :]
        mine = slice(at, at + n)
        o_p[0, mine, :] = carried[RADIUS : RADIUS + n, 0:cols] / ep[at + EDGE : at + EDGE + n, 0:cols]
        o_s[0, mine, :] = col_pass(row_pass(-carried / first[span, :], n), cols)

    moving = {}
    joined = 0
    ahead = 2 if bits == 2 else count
    for i, c in enumerate(order):
        lifted(c)
        if 0 < i <= ahead:
            moving[order[i - 1]] = join(order[i - 1], 0, moving[order[i - 1]])
            joined = i
        moving[c] = logs(c)
    if joined < ahead:
        for c in order[joined:]:
            moving[c] = join(c, 0, moving[c])
        joined = count
    for bit in range(1, bits - 1):
        for c in order:
            moving[c] = join(c, bit, moving[c])
    areas = regions(rows)
    mains, corners = {}, []
    for i, c in enumerate(order):
        if bits > 1:
            moving[c] = join(c, bits - 1, moving[c])
        if joined < count:
            moving[order[joined]] = join(order[joined], 0, moving[order[joined]])
            joined += 1
        mains[c], corner = second(c, moving[c])
        corners += corner
        if i == 2:
            take_main(order[0], mains[order[0]])
            take_main(order[1], mains[order[1]])
            take_corners(corners)
            backward(*areas[0])
            backward(*areas[1])
        if i > 2:
            take_main(order[i - 1], mains[order[i - 1]])
            backward(*areas[i - 1])
    take_main(order[-1], mains[order[-1]])
    backward(*areas[-1])
    for copy in sent:
        copy.wait_send()


def write_out(p_ref, s_ref, p_out, s_out, done):
    copies = [
        pltpu.make_async_copy(p_ref, p_out, done.at[0]),
        pltpu.make_async_copy(s_ref, s_out, done.at[1]),
    ]
    for copy in copies:
        copy.start()
    for copy in copies:
        copy.wait()


def per_device(n_hour, n_lat, n_lon, precip, scaling, hour_weight, cotangent):
    rows, cols = precip.shape[1:]
    tall, wide, lanes = rows + 2 * EDGE, cols + STEP, rows + 2 * STEP
    bits = n_hour.bit_length() - 1
    pieces, _ = plan(rows)
    count = len(pieces)
    assert n_hour == 1 << bits and bits > 0 and min(n_lat, n_lon) > 1
    assert rows % STEP == 0 and cols % (2 * STEP) == 0 and count > 3
    ext, tile = pltpu.VMEM((tall, wide), F32), pltpu.VMEM((rows, cols), F32)
    pair = pltpu.VMEM((2, rows, cols), F32)
    steps = pltpu.VMEM((max(bits - 1, 1), rows, cols), F32)
    copies = 10 + count * (bits + 3) + 6
    out = jax.ShapeDtypeStruct(precip.shape, F32)
    hbm = pl.BlockSpec(memory_space=pl.ANY)
    vmem = pl.BlockSpec(memory_space=pltpu.VMEM)
    held = pltpu.VMEM(precip.shape, F32)
    stage, halo = pltpu.VMEM((EDGE + RADIUS, rows), F32), pltpu.VMEM((EDGE + RADIUS, lanes), F32)
    piece_stage, piece_halo = pltpu.VMEM((count, EDGE, STEP), F32), pltpu.VMEM((count + 2, EDGE, STEP), F32)
    spare = 64 * 2**20 - 2 * 4 * rows * cols - 2**19
    grads = pl.pallas_call(
        functools.partial(kernel, (n_hour, n_lat, n_lon, rows, cols)),
        out_shape=(held, held),
        in_specs=[hbm, hbm, pl.BlockSpec(memory_space=pltpu.SMEM), hbm],
        out_specs=(vmem, vmem),
        scratch_shapes=[
            ext, ext, tile, ext, ext, ext, pair, tile, steps, steps, pair, tile,
            stage, stage, halo, halo, piece_stage, piece_stage, piece_halo, piece_halo,
            pltpu.VMEM((8 * STEP, 2 * STEP), BF16), pltpu.VMEM((5 * STEP, STEP), BF16),
            pltpu.SemaphoreType.DMA((7,)),
            pltpu.SemaphoreType.DMA((copies,)), pltpu.SemaphoreType.DMA((copies,)),
        ] + [pltpu.VMEM((n, 3 * (n + EDGE)), BF16) for n in heights(rows)],
        compiler_params=pltpu.CompilerParams(
            collective_id=0, has_side_effects=True, vmem_limit_bytes=spare
        ),
    )(precip, scaling, hour_weight, cotangent)
    return pl.pallas_call(
        write_out,
        out_shape=(out, out),
        in_specs=[vmem, vmem],
        out_specs=(hbm, hbm),
        scratch_shapes=[pltpu.SemaphoreType.DMA((2,))],
    )(*grads)


def solution(mesh):
    field = P("hour", "lat", "lon")
    sizes = [mesh.shape[a] for a in ("hour", "lat", "lon")]
    return jax.shard_map(
        functools.partial(per_device, *sizes), mesh=mesh,
        in_specs=(field, field, P("hour"), field), out_specs=(field, field), check_vma=False,
    )
```

```python
import functools
import math
import jax
import jax.numpy as jnp
from jax import lax
from jax.experimental import pallas as pl
from jax.experimental.pallas import tpu as pltpu
from jax.sharding import PartitionSpec as P

RADIUS = 8
PHI = 0.8
SPREAD = 50.0
STEP = 128
EDGE = 2 * RADIUS
TOTAL = sum(math.exp(-d * d / SPREAD) for d in range(-RADIUS, RADIUS + 1))
MESH = pl.DeviceIdType.MESH
F32, BF16 = jnp.float32, jnp.bfloat16


def split(x):
    high = x.astype(BF16)
    return high, (x - high.astype(F32)).astype(BF16)


def taps(d):
    d = d.astype(F32)
    return jnp.where(jnp.abs(d) <= RADIUS, jnp.exp(-d * d / SPREAD) / TOTAL, 0.0)


def either(k, low):
    high = k.astype(BF16).astype(F32)
    return jnp.where(low, k - high, high).astype(BF16)


def places(rows, cols):
    return [lax.broadcasted_iota(jnp.int32, (rows, cols), at) for at in (0, 1)]


def stacked_rows(n):
    depth = n + EDGE
    i, j = places(n, 3 * depth)
    third = j >= 2 * depth
    at = jnp.where(third, j - 2 * depth, jnp.where(j >= depth, j - depth, j))
    return either(taps(at - i - RADIUS), third)


def stacked_cols(size):
    i, j = places(size, size)
    high, low = split(taps(i - j))
    i, j = places(2 * STEP, size)
    middle = (i >= STEP + STEP // 4) & (i < STEP + 3 * STEP // 4)
    lane = jnp.where(i >= STEP, i - STEP, i)
    lane = jnp.where(middle, jnp.where(lane >= STEP // 2, lane - STEP // 2, lane + STEP // 2), lane)
    near = taps(jnp.where(lane >= STEP // 2, lane - STEP, lane + size) - j)
    return jnp.concatenate([high, high, low, either(near, middle)], axis=0)


def row_pass(weights, x):
    high, low = split(x)
    return jnp.dot(weights[...], jnp.concatenate([high, low, high], axis=0), preferred_element_type=F32)


def col_pass(pair, last, x, width):
    high, low = split(x)
    blocks = x.shape[1] // STEP
    lane = lax.broadcasted_iota(jnp.int32, (x.shape[0], STEP), 1)
    middle = (lane >= STEP // 4) & (lane < 3 * STEP // 4)
    out = []
    for start in range(0, width, 2 * STEP):
        size = min(2 * STEP, width - start)
        before = (start // STEP - 1) % blocks * STEP
        after = (start + size) // STEP % blocks * STEP
        beside = jnp.where(lane >= STEP // 2, x[:, before : before + STEP], x[:, after : after + STEP])
        near = beside.astype(BF16)
        rounded = near.astype(F32)
        mixed = jnp.where(middle, pltpu.roll(rounded, STEP // 2, 1), beside - rounded).astype(BF16)
        h, l = high[:, start : start + size], low[:, start : start + size]
        weights = pair if size == 2 * STEP else last
        out.append(jnp.dot(
            jnp.concatenate([h, l, h, near, mixed], axis=1), weights[...], preferred_element_type=F32
        ))
    return jnp.concatenate(out, axis=1)


def backward(at, n, refs, bands):
    ds, first, lift, ep, pair, last = refs
    cols = ds.shape[1] - STEP
    span = slice(at + RADIUS, at + n + 3 * RADIUS)
    d = col_pass(pair, last, row_pass(bands[n + EDGE], ds[at : at + n + 2 * EDGE, :]), ds.shape[1])
    carried = PHI * d * lift[span, :]
    out = carried[RADIUS : RADIUS + n, 0:cols] / ep[at + EDGE : at + EDGE + n, 0:cols]
    return out, col_pass(pair, last, row_pass(bands[n], -carried / first[span, :]), cols)


def plan(rows):
    sizes = [STEP // 2] + [STEP] * ((rows - 2 * STEP) // STEP) + [STEP // 2, STEP]
    pieces = [(sum(sizes[:i]), n) for i, n in enumerate(sizes)]
    last = len(pieces) - 1
    return pieces, [0, last] + list(range(1, last))


def heights(rows):
    found = set()
    pieces, _ = plan(rows)
    for _, n in pieces:
        found |= {n, n + EDGE}
    for _, n in regions(rows):
        found |= {n, n + EDGE}
    return sorted(found)


def regions(rows):
    pieces, order = plan(rows)
    last = len(pieces) - 1
    found = [(0, pieces[0][1] - EDGE), (pieces[last][0] + EDGE, pieces[last][1] - EDGE)]
    at = found[0][1]
    for c in order[2:]:
        end = sum(pieces[c]) + (EDGE if c == last - 1 else -EDGE)
        found.append((at, end - at))
        at = end
    return found


def kernel(sizes, p_hbm, s_hbm, w_ref, c_hbm, *refs):
    heads = heights(sizes[3])
    o_p, o_s, ds, first, lift, ep, *refs = refs
    weights, refs = refs[: 2 + len(heads)], refs[2 + len(heads) :]
    (es, ct, own, got, part, other, both, scale,
     st_l, st_r, h_l, h_r, sd_l, sd_r, hd_l, hd_r, local, sends, recvs) = refs
    t_pair, t_last, *bands = weights
    n_hour, n_lat, n_lon, rows, cols = sizes
    pieces, order = plan(rows)
    count = len(pieces)
    by_height = dict(zip(heads, bands))
    held = (ds, first, lift, ep, t_pair, t_last)
    tall, wide = rows + 2 * EDGE, cols + STEP
    bits = n_hour.bit_length() - 1
    hour, lat, lon = (lax.axis_index(a) for a in ("hour", "lat", "lon"))
    side = lax.rem(hour, 2)
    up, down = lax.rem(lat + n_lat - 1, n_lat), lax.rem(lat + 1, n_lat)
    left, right = lax.rem(lon + n_lon - 1, n_lon), lax.rem(lon + 1, n_lon)

    def flip(bit):
        m = 1 << bit
        return hour + m - 2 * m * lax.rem(hour // m, 2)

    own_rows = pl.ds(EDGE, rows)
    loads = []
    for z, n in ((0, STEP), (cols - STEP, STEP), (STEP, cols - 2 * STEP)):
        for src, dst in ((s_hbm, es), (p_hbm, ep)):
            lanes = pl.ds(z, n)
            loads.append(pltpu.make_async_copy(src.at[0, :, lanes], dst.at[own_rows, lanes], local.at[len(loads)]))
    loads.append(pltpu.make_async_copy(c_hbm.at[0], ct, local.at[len(loads)]))
    for copy in loads:
        copy.start()

    barrier = pltpu.get_barrier_semaphore()
    lats = [up, down] if n_lat > 2 else [down]
    lons = [left, right] if n_lon > 2 else [right]
    peers = [{"lon": z} for z in lons] + [{"lat": x} for x in lats]
    peers += [{"lat": x, "lon": z} for x in lats for z in lons]
    peers += [{"hour": flip(bit)} for bit in range(bits)]
    for peer in peers:
        pl.semaphore_signal(barrier, inc=1, device_id=peer, device_id_type=MESH)

    sd_l[...] = jnp.zeros_like(sd_l)
    sd_r[...] = jnp.zeros_like(sd_r)
    pl.semaphore_wait(barrier, len(peers))

    sent = []

    def send(src, dst, peer):
        at = len(sent)
        copy = pltpu.make_async_remote_copy(
            src_ref=src, dst_ref=dst, send_sem=sends.at[at], recv_sem=recvs.at[at],
            device_id=peer, device_id_type=MESH,
        )
        copy.start()
        sent.append(copy)
        return copy

    def fill(at, n):
        r, lanes = slice(EDGE + at, EDGE + at + n), slice(at, at + n)
        st_l[0:EDGE, lanes] = es[r, 0:STEP].T[0:EDGE]
        st_r[0:EDGE, lanes] = es[r, cols - STEP : cols].T[STEP - EDGE :]
        st_l[EDGE:, lanes] = ep[r, 0:STEP].T[0:RADIUS]
        st_r[EDGE:, lanes] = ep[r, cols - STEP : cols].T[STEP - RADIUS :]

    early, late = [], []
    for src, dst in ((s_hbm, es), (p_hbm, ep)):
        early.append(send(src.at[0, pl.ds(rows - EDGE, EDGE)], dst.at[pl.ds(0, EDGE), pl.ds(0, cols)], {"lat": down}))
    for copy in loads[:4]:
        copy.wait()
    fill(0, STEP)
    fill(rows - STEP, STEP)
    first_lanes, last_lanes = pl.ds(0, STEP), pl.ds(rows - STEP, STEP)
    sides = ((st_l, h_r, left), (st_r, h_l, right))
    for stage, dst, z in sides:
        early.append(send(stage.at[:, first_lanes], dst.at[:, pl.ds(STEP, STEP)], {"lon": z}))
        early.append(send(stage.at[:, last_lanes], dst.at[:, first_lanes], {"lat": down, "lon": z}))
    fill(STEP, rows - 2 * STEP)
    for stage, dst, z in sides:
        late.append(send(stage.at[:, first_lanes], dst.at[:, pl.ds(STEP + rows, STEP)], {"lat": up, "lon": z}))
        late.append(send(stage.at[:, pl.ds(STEP, rows - STEP)], dst.at[:, pl.ds(2 * STEP, rows - STEP)], {"lon": z}))
    for src, dst in ((s_hbm, es), (p_hbm, ep)):
        late.append(send(src.at[0, pl.ds(0, EDGE)], dst.at[pl.ds(EDGE + rows, EDGE), pl.ds(0, cols)], {"lat": up}))

    top, bottom = slice(0, EDGE), slice(EDGE + rows, tall)

    def beside(at, n, start, skip, size):
        lanes = slice(at, at + n)
        for dst, low, high in ((es, 0, EDGE), (ep, EDGE, EDGE + RADIUS)):
            ones = jnp.ones((STEP - 2 * (high - low), n), F32)
            block = jnp.concatenate([h_r[low:high, lanes], ones, h_l[low:high, lanes]], axis=0).T
            dst[start : start + size, cols:wide] = block[skip : skip + size]

    weight = w_ref[0]
    t_pair[...] = stacked_cols(2 * STEP)
    t_last[...] = stacked_cols(STEP)
    for n, ref in by_height.items():
        ref[...] = stacked_rows(n)
    for copy in loads[4:]:
        copy.wait()
    for copy in early:
        copy.wait_recv()
    beside(0, 2 * STEP, 0, STEP - EDGE, STEP + EDGE)
    es[top, :] = jnp.where(lat > 0, es[top, :], 0.0)

    def rest():
        for copy in late:
            copy.wait_recv()
        beside(2 * STEP, rows, STEP + EDGE, 0, rows - STEP + EDGE)
        es[bottom, :] = jnp.where(lat < n_lat - 1, es[bottom, :], 0.0)

    def lifted(c):
        at, n = pieces[c]
        span = slice(at + RADIUS, at + RADIUS + n + EDGE)
        a = col_pass(t_pair, t_last, row_pass(by_height[n + EDGE], es[at : at + n + 2 * EDGE, :]), wide)
        first[span, :] = a
        u = jnp.exp(PHI * jnp.log(ep[span, :] / a))
        if c == 0 or c == count - 1:
            e = lax.broadcasted_iota(jnp.int32, u.shape, 0) + (at + RADIUS)
            inside = ((lat > 0) | (e >= EDGE)) & ((lat < n_lat - 1) | (e < EDGE + rows))
            u = jnp.where(inside, u, 0.0)
        lift[span, :] = u

    def logs(c):
        at, n = pieces[c]
        b = col_pass(t_pair, t_last, row_pass(by_height[n], lift[at + RADIUS : at + RADIUS + n + EDGE, :]), cols)
        logb = jnp.log(b)
        mine = slice(at, at + n)
        own[0, mine, :] = weight * logb
        own[1, mine, :] = ct[mine, :] * jnp.exp(-PHI * logb)
        scale[mine, :] = PHI / b
        r = pl.ds(at, n)
        return send(own.at[1 - side, r], got.at[r], {"hour": flip(0)})

    def join(c, bit, copy):
        copy.wait_recv()
        at, n = pieces[c]
        mine = slice(at, at + n)
        r = pl.ds(at, n)
        if bit == 0:
            value = own[side, mine, :] + got[mine, :]
        else:
            value = part[bit - 1, mine, :] + other[bit - 1, mine, :]
        if bit == bits - 1:
            both[side, mine, :] = value
            return send(both.at[side, r], both.at[side, r], {"hour": flip(0)})
        part[bit, mine, :] = value
        return send(part.at[bit, r], other.at[bit, r], {"hour": flip(bit + 1)})

    def second(c, copy):
        copy.wait_recv()
        at, n = pieces[c]
        mine = slice(at, at + n)
        d = jnp.exp(PHI * both[0, mine, :]) * (weight * both[1, mine, :] - own[1, mine, :]) * scale[mine, :]
        ds[at + EDGE : at + EDGE + n, 0:cols] = d
        sd_l[c, :, 0:n] = d[:, 0:STEP].T[0:EDGE]
        sd_r[c, :, 0:n] = d[:, cols - STEP : cols].T[STEP - EDGE :]
        main, corner = [], []
        inner = pl.ds(0, cols)
        if c == 0:
            corner.append(send(ds.at[pl.ds(EDGE, EDGE), inner], ds.at[pl.ds(EDGE + rows, EDGE), inner], {"lat": up}))
        if c == count - 1:
            corner.append(send(ds.at[pl.ds(rows, EDGE), inner], ds.at[pl.ds(0, EDGE), inner], {"lat": down}))
        for stage, dst, z in ((sd_l, hd_r, left), (sd_r, hd_l, right)):
            main.append(send(stage.at[c], dst.at[c + 1], {"lon": z}))
            if c == 0:
                corner.append(send(stage.at[c], dst.at[count + 1], {"lat": up, "lon": z}))
            if c == count - 1:
                corner.append(send(stage.at[c], dst.at[0], {"lat": down, "lon": z}))
        return main, corner

    def side_block(i, n):
        zeros = jnp.zeros((STEP - 2 * EDGE, n), F32)
        return jnp.concatenate([hd_r[i, :, 0:n], zeros, hd_l[i, :, 0:n]], axis=0).T

    def take_main(c, copies):
        for copy in copies:
            copy.wait_recv()
        at, n = pieces[c]
        ds[EDGE + at : EDGE + at + n, cols:wide] = side_block(c + 1, n)

    def take_corners(copies):
        for copy in copies:
            copy.wait_recv()
        n = pieces[count - 1][1]
        ds[top, cols:wide] = side_block(0, n)[n - EDGE :]
        ds[bottom, cols:wide] = side_block(count + 1, pieces[0][1])[0:EDGE]
        ds[top, :] = jnp.where(lat > 0, ds[top, :], 0.0)
        ds[bottom, :] = jnp.where(lat < n_lat - 1, ds[bottom, :], 0.0)

    def finish(at, n):
        mine = slice(at, at + n)
        o_p[0, mine, :], o_s[0, mine, :] = backward(at, n, held, by_height)

    moving = {}
    joined = 0
    ahead = 3 if bits == 2 else count
    for i, c in enumerate(order):
        lifted(c)
        if 0 < i <= ahead:
            moving[order[i - 1]] = join(order[i - 1], 0, moving[order[i - 1]])
            joined = i
        moving[c] = logs(c)
        if i == 0:
            rest()
    if joined < ahead:
        for c in order[joined:]:
            moving[c] = join(c, 0, moving[c])
        joined = count
    for bit in range(1, bits - 1):
        for c in order:
            moving[c] = join(c, bit, moving[c])
    areas = regions(rows)
    mains, corners = {}, []
    for i, c in enumerate(order):
        if bits > 1:
            moving[c] = join(c, bits - 1, moving[c])
        if joined < count:
            moving[order[joined]] = join(order[joined], 0, moving[order[joined]])
            joined += 1
        mains[c], corner = second(c, moving[c])
        corners += corner
        if i == 2:
            take_main(order[0], mains[order[0]])
            take_main(order[1], mains[order[1]])
            take_corners(corners)
            finish(*areas[0])
            finish(*areas[1])
        if i > 2:
            take_main(order[i - 1], mains[order[i - 1]])
            finish(*areas[i - 1])
    take_main(order[-1], mains[order[-1]])
    for copy in sent:
        copy.wait_send()


def write_out(area, p_ref, s_ref, ds, first, lift, ep, t_pair, t_last, low, high, p_out, s_out, p_last, s_last, done):
    at, n = area
    rows = p_ref.shape[1]
    copies = []

    def write(src, dst):
        copies.append(pltpu.make_async_copy(src, dst, done.at[len(copies)]))
        copies[-1].start()

    for r in (pl.ds(0, at), pl.ds(at + n, rows - at - n)):
        write(p_ref.at[0, r], p_out.at[0, r])
        write(s_ref.at[0, r], s_out.at[0, r])
    refs = (ds, first, lift, ep, t_pair, t_last)
    p_last[...], s_last[...] = backward(at, n, refs, {n: low, n + EDGE: high})
    write(p_last, p_out.at[0, pl.ds(at, n)])
    write(s_last, s_out.at[0, pl.ds(at, n)])
    for copy in copies:
        copy.wait()


def per_device(n_hour, n_lat, n_lon, precip, scaling, hour_weight, cotangent):
    rows, cols = precip.shape[1:]
    tall, wide, lanes = rows + 2 * EDGE, cols + STEP, rows + 2 * STEP
    bits = n_hour.bit_length() - 1
    pieces, _ = plan(rows)
    count = len(pieces)
    assert n_hour == 1 << bits and bits > 0 and min(n_lat, n_lon) > 1
    assert rows % STEP == 0 and cols % (2 * STEP) == 0 and count > 3
    ext, tile = pltpu.VMEM((tall, wide), F32), pltpu.VMEM((rows, cols), F32)
    pair = pltpu.VMEM((2, rows, cols), F32)
    steps = pltpu.VMEM((max(bits - 1, 1), rows, cols), F32)
    copies = 12 + count * (bits + 3) + 6
    out = jax.ShapeDtypeStruct(precip.shape, F32)
    hbm = pl.BlockSpec(memory_space=pl.ANY)
    vmem = pl.BlockSpec(memory_space=pltpu.VMEM)
    held = pltpu.VMEM(precip.shape, F32)
    stage, halo = pltpu.VMEM((EDGE + RADIUS, rows), F32), pltpu.VMEM((EDGE + RADIUS, lanes), F32)
    piece_stage, piece_halo = pltpu.VMEM((count, EDGE, STEP), F32), pltpu.VMEM((count + 2, EDGE, STEP), F32)
    heads = heights(rows)
    fixed = [(8 * STEP, 2 * STEP), (5 * STEP, STEP)] + [(n, 3 * (n + EDGE)) for n in heads]
    held = [pltpu.VMEM(precip.shape, F32)] * 2 + [ext] * 4 + [pltpu.VMEM(k, BF16) for k in fixed]
    size = 4 * (2 * rows * cols + 4 * tall * wide) + sum(2 * k[0] * (-(-k[1] // STEP) * STEP) for k in fixed)
    spare = (64 * 2**20 - size - 2**19) // 1024 * 1024
    made = pl.pallas_call(
        functools.partial(kernel, (n_hour, n_lat, n_lon, rows, cols)),
        out_shape=tuple(held),
        in_specs=[hbm, hbm, pl.BlockSpec(memory_space=pltpu.SMEM), hbm],
        out_specs=tuple([vmem] * len(held)),
        scratch_shapes=[
            ext, tile, pair, tile, steps, steps, pair, tile,
            stage, stage, halo, halo, piece_stage, piece_stage, piece_halo, piece_halo,
            pltpu.SemaphoreType.DMA((7,)),
            pltpu.SemaphoreType.DMA((copies,)), pltpu.SemaphoreType.DMA((copies,)),
        ],
        compiler_params=pltpu.CompilerParams(
            collective_id=0, has_side_effects=True, vmem_limit_bytes=spare
        ),
    )(precip, scaling, hour_weight, cotangent)
    at, n = regions(rows)[-1]
    bands = dict(zip(heads, made[8:]))
    return pl.pallas_call(
        functools.partial(write_out, (at, n)),
        out_shape=(out, out),
        in_specs=[vmem] * 10,
        out_specs=(hbm, hbm),
        scratch_shapes=[
            pltpu.VMEM((n, cols), F32), pltpu.VMEM((n, cols), F32), pltpu.SemaphoreType.DMA((6,)),
        ],
        compiler_params=pltpu.CompilerParams(vmem_limit_bytes=8 * 2**20),
    )(*made[:8], bands[n], bands[n + EDGE])


def solution(mesh):
    field = P("hour", "lat", "lon")
    sizes = [mesh.shape[a] for a in ("hour", "lat", "lon")]
    return jax.shard_map(
        functools.partial(per_device, *sizes), mesh=mesh,
        in_specs=(field, field, P("hour"), field), out_specs=(field, field), check_vma=False,
    )
```

```python
import functools
import math
import jax
import jax.numpy as jnp
from jax import lax
from jax.experimental import pallas as pl
from jax.experimental.pallas import tpu as pltpu
from jax.sharding import PartitionSpec as P

RADIUS = 8
PHI = 0.8
SPREAD = 50.0
STEP = 128
PART = STEP // 2
EDGE = 2 * RADIUS
TOTAL = sum(math.exp(-d * d / SPREAD) for d in range(-RADIUS, RADIUS + 1))
MESH = pl.DeviceIdType.MESH
F32, BF16 = jnp.float32, jnp.bfloat16


def split(x):
    high = x.astype(BF16)
    return high, (x - high.astype(F32)).astype(BF16)


def taps(d):
    d = d.astype(F32)
    return jnp.where(jnp.abs(d) <= RADIUS, jnp.exp(-d * d / SPREAD) / TOTAL, 0.0)


def either(k, low):
    high = k.astype(BF16).astype(F32)
    return jnp.where(low, k - high, high).astype(BF16)


def places(rows, cols):
    return [lax.broadcasted_iota(jnp.int32, (rows, cols), at) for at in (0, 1)]


def stacked_rows(n):
    depth = n + EDGE
    i, j = places(n, 3 * depth)
    third = j >= 2 * depth
    at = jnp.where(third, j - 2 * depth, jnp.where(j >= depth, j - depth, j))
    return either(taps(at - i - RADIUS), third)


def stacked_cols(size):
    i, j = places(size, size)
    high, low = split(taps(i - j))
    i, j = places(2 * STEP, size)
    middle = (i >= STEP + STEP // 4) & (i < STEP + 3 * STEP // 4)
    lane = jnp.where(i >= STEP, i - STEP, i)
    lane = jnp.where(middle, jnp.where(lane >= STEP // 2, lane - STEP // 2, lane + STEP // 2), lane)
    near = taps(jnp.where(lane >= STEP // 2, lane - STEP, lane + size) - j)
    return jnp.concatenate([high, high, low, either(near, middle)], axis=0)


def row_pass(weights, x):
    high, low = split(x)
    return jnp.dot(weights[...], jnp.concatenate([high, low, high], axis=0), preferred_element_type=F32)


def col_pass(pair, last, x, width):
    high, low = split(x)
    blocks = x.shape[1] // STEP
    lane = lax.broadcasted_iota(jnp.int32, (x.shape[0], STEP), 1)
    middle = (lane >= STEP // 4) & (lane < 3 * STEP // 4)
    out = []
    for start in range(0, width, 2 * STEP):
        size = min(2 * STEP, width - start)
        before = (start // STEP - 1) % blocks * STEP
        after = (start + size) // STEP % blocks * STEP
        beside = jnp.where(lane >= STEP // 2, x[:, before : before + STEP], x[:, after : after + STEP])
        near = beside.astype(BF16)
        rounded = near.astype(F32)
        mixed = jnp.where(middle, pltpu.roll(rounded, STEP // 2, 1), beside - rounded).astype(BF16)
        h, l = high[:, start : start + size], low[:, start : start + size]
        weights = pair if size == 2 * STEP else last
        out.append(jnp.dot(
            jnp.concatenate([h, l, h, near, mixed], axis=1), weights[...], preferred_element_type=F32
        ))
    return jnp.concatenate(out, axis=1)


def backward(at, n, refs, bands):
    ds, first, lift, ep, pair, last = refs
    cols = ds.shape[1] - STEP
    span = slice(at + RADIUS, at + n + 3 * RADIUS)
    d = col_pass(pair, last, row_pass(bands[n + EDGE], ds[at : at + n + 2 * EDGE, :]), ds.shape[1])
    carried = PHI * d * lift[span, :]
    out = carried[RADIUS : RADIUS + n, 0:cols] / ep[at + EDGE : at + EDGE + n, 0:cols]
    return out, col_pass(pair, last, row_pass(bands[n], -carried / first[span, :]), cols)


def plan(rows):
    sizes = [STEP // 2] + [STEP] * ((rows - 2 * STEP) // STEP) + [STEP // 2, STEP]
    pieces = [(sum(sizes[:i]), n) for i, n in enumerate(sizes)]
    last = len(pieces) - 1
    return pieces, [0, last] + list(range(1, last))


def split_up(rows):
    pieces, order = plan(rows)
    found = []
    for c in order:
        at, n = pieces[c]
        own = list(range(at // PART, (at + n) // PART))
        found += own[::-1] if c == len(pieces) - 1 else own
    return found


def made_by(rows):
    pieces, order = plan(rows)
    found, at = [], -1
    for c in order:
        at += pieces[c][1] // PART
        found.append(at)
    return found


def heights(rows):
    found = set()
    spans = plan(rows)[0] + regions(rows)
    spans.append((0, spans[-2][1] // 2))
    for _, n in spans:
        found |= {n, n + EDGE}
    return sorted(found)


def regions(rows):
    pieces, order = plan(rows)
    last = len(pieces) - 1
    found = [(0, pieces[0][1] - EDGE), (pieces[last][0] + EDGE, pieces[last][1] - EDGE)]
    at = found[0][1]
    for c in order[2:]:
        end = sum(pieces[c]) + (EDGE if c == last - 1 else -EDGE)
        found.append((at, end - at))
        at = end
    return found


def kernel(sizes, p_hbm, s_hbm, w_ref, c_hbm, *refs):
    heads = heights(sizes[3])
    o_p, o_s, ds, first, lift, ep, *refs = refs
    weights, refs = refs[: 2 + len(heads)], refs[2 + len(heads) :]
    (es, ct, own, got, part, other, both, scale,
     st_l, st_r, h_l, h_r, sd_l, sd_r, hd_l, hd_r, local, sends, recvs) = refs
    t_pair, t_last, *bands = weights
    n_hour, n_lat, n_lon, rows, cols = sizes
    pieces, order = plan(rows)
    parts = split_up(rows)
    count = len(parts)
    by_height = dict(zip(heads, bands))
    held = (ds, first, lift, ep, t_pair, t_last)
    tall, wide = rows + 2 * EDGE, cols + STEP
    bits = n_hour.bit_length() - 1
    hour, lat, lon = (lax.axis_index(a) for a in ("hour", "lat", "lon"))
    side = lax.rem(hour, 2)
    up, down = lax.rem(lat + n_lat - 1, n_lat), lax.rem(lat + 1, n_lat)
    left, right = lax.rem(lon + n_lon - 1, n_lon), lax.rem(lon + 1, n_lon)

    def flip(bit):
        m = 1 << bit
        return hour + m - 2 * m * lax.rem(hour // m, 2)

    own_rows = pl.ds(EDGE, rows)
    loads = []
    for z, n in ((0, STEP), (cols - STEP, STEP), (STEP, cols - 2 * STEP)):
        for src, dst in ((s_hbm, es), (p_hbm, ep)):
            lanes = pl.ds(z, n)
            loads.append(pltpu.make_async_copy(src.at[0, :, lanes], dst.at[own_rows, lanes], local.at[len(loads)]))
    loads.append(pltpu.make_async_copy(c_hbm.at[0], ct, local.at[len(loads)]))
    for copy in loads:
        copy.start()

    barrier = pltpu.get_barrier_semaphore()
    lats = [up, down] if n_lat > 2 else [down]
    lons = [left, right] if n_lon > 2 else [right]
    peers = [{"lon": z} for z in lons] + [{"lat": x} for x in lats]
    peers += [{"lat": x, "lon": z} for x in lats for z in lons]
    peers += [{"hour": flip(bit)} for bit in range(bits)]
    for peer in peers:
        pl.semaphore_signal(barrier, inc=1, device_id=peer, device_id_type=MESH)

    sd_l[...] = jnp.zeros_like(sd_l)
    sd_r[...] = jnp.zeros_like(sd_r)
    pl.semaphore_wait(barrier, len(peers))

    sent = []

    def send(src, dst, peer):
        at = len(sent)
        copy = pltpu.make_async_remote_copy(
            src_ref=src, dst_ref=dst, send_sem=sends.at[at], recv_sem=recvs.at[at],
            device_id=peer, device_id_type=MESH,
        )
        copy.start()
        sent.append(copy)
        return copy

    def fill(at, n):
        r, lanes = slice(EDGE + at, EDGE + at + n), slice(at, at + n)
        st_l[0:EDGE, lanes] = es[r, 0:STEP].T[0:EDGE]
        st_r[0:EDGE, lanes] = es[r, cols - STEP : cols].T[STEP - EDGE :]
        st_l[EDGE:, lanes] = ep[r, 0:STEP].T[0:RADIUS]
        st_r[EDGE:, lanes] = ep[r, cols - STEP : cols].T[STEP - RADIUS :]

    early, late = [], []
    for src, dst in ((s_hbm, es), (p_hbm, ep)):
        early.append(send(src.at[0, pl.ds(rows - EDGE, EDGE)], dst.at[pl.ds(0, EDGE), pl.ds(0, cols)], {"lat": down}))
    for copy in loads[:4]:
        copy.wait()
    fill(0, STEP)
    fill(rows - STEP, STEP)
    first_lanes, last_lanes = pl.ds(0, STEP), pl.ds(rows - STEP, STEP)
    sides = ((st_l, h_r, left), (st_r, h_l, right))
    for stage, dst, z in sides:
        early.append(send(stage.at[:, first_lanes], dst.at[:, pl.ds(STEP, STEP)], {"lon": z}))
        early.append(send(stage.at[:, last_lanes], dst.at[:, first_lanes], {"lat": down, "lon": z}))
    fill(STEP, rows - 2 * STEP)
    for stage, dst, z in sides:
        late.append(send(stage.at[:, first_lanes], dst.at[:, pl.ds(STEP + rows, STEP)], {"lat": up, "lon": z}))
        late.append(send(stage.at[:, pl.ds(STEP, rows - STEP)], dst.at[:, pl.ds(2 * STEP, rows - STEP)], {"lon": z}))
    for src, dst in ((s_hbm, es), (p_hbm, ep)):
        late.append(send(src.at[0, pl.ds(0, EDGE)], dst.at[pl.ds(EDGE + rows, EDGE), pl.ds(0, cols)], {"lat": up}))

    top, bottom = slice(0, EDGE), slice(EDGE + rows, tall)

    def beside(at, n, start, skip, size):
        lanes = slice(at, at + n)
        for dst, low, high in ((es, 0, EDGE), (ep, EDGE, EDGE + RADIUS)):
            ones = jnp.ones((STEP - 2 * (high - low), n), F32)
            block = jnp.concatenate([h_r[low:high, lanes], ones, h_l[low:high, lanes]], axis=0).T
            dst[start : start + size, cols:wide] = block[skip : skip + size]

    weight = w_ref[0]
    t_pair[...] = stacked_cols(2 * STEP)
    t_last[...] = stacked_cols(STEP)
    for n, ref in by_height.items():
        ref[...] = stacked_rows(n)
    for copy in loads[4:]:
        copy.wait()
    for copy in early:
        copy.wait_recv()
    beside(0, 2 * STEP, 0, STEP - EDGE, STEP + EDGE)
    es[top, :] = jnp.where(lat > 0, es[top, :], 0.0)

    def rest():
        for copy in late:
            copy.wait_recv()
        beside(2 * STEP, rows, STEP + EDGE, 0, rows - STEP + EDGE)
        es[bottom, :] = jnp.where(lat < n_lat - 1, es[bottom, :], 0.0)

    def lifted(c):
        at, n = pieces[c]
        span = slice(at + RADIUS, at + RADIUS + n + EDGE)
        a = col_pass(t_pair, t_last, row_pass(by_height[n + EDGE], es[at : at + n + 2 * EDGE, :]), wide)
        first[span, :] = a
        u = jnp.exp(PHI * jnp.log(ep[span, :] / a))
        if c == 0 or c == len(pieces) - 1:
            e = lax.broadcasted_iota(jnp.int32, u.shape, 0) + (at + RADIUS)
            inside = ((lat > 0) | (e >= EDGE)) & ((lat < n_lat - 1) | (e < EDGE + rows))
            u = jnp.where(inside, u, 0.0)
        lift[span, :] = u

    def logs(c):
        at, n = pieces[c]
        b = col_pass(t_pair, t_last, row_pass(by_height[n], lift[at + RADIUS : at + RADIUS + n + EDGE, :]), cols)
        logb = jnp.log(b)
        mine = slice(at, at + n)
        own[0, mine, :] = weight * logb
        own[1, mine, :] = ct[mine, :] * jnp.exp(-PHI * logb)
        scale[mine, :] = PHI / b
        for i, q in enumerate(parts):
            if at <= q * PART < at + n:
                r = pl.ds(q * PART, PART)
                moving[i] = send(own.at[1 - side, r], got.at[r], {"hour": flip(0)})

    def join(i, bit):
        moving[i].wait_recv()
        at = parts[i] * PART
        mine = slice(at, at + PART)
        r = pl.ds(at, PART)
        if bit == 0:
            value = own[side, mine, :] + got[mine, :]
        else:
            value = part[bit - 1, mine, :] + other[bit - 1, mine, :]
        if bit == bits - 1:
            both[side, mine, :] = value
            moving[i] = send(both.at[side, r], both.at[side, r], {"hour": flip(0)})
            return
        part[bit, mine, :] = value
        moving[i] = send(part.at[bit, r], other.at[bit, r], {"hour": flip(bit + 1)})

    def second(i):
        moving[i].wait_recv()
        c = parts[i]
        at, n = c * PART, PART
        mine = slice(at, at + n)
        d = jnp.exp(PHI * both[0, mine, :]) * (weight * both[1, mine, :] - own[1, mine, :]) * scale[mine, :]
        ds[at + EDGE : at + EDGE + n, 0:cols] = d
        sd_l[c, :, 0:n] = d[:, 0:STEP].T[0:EDGE]
        sd_r[c, :, 0:n] = d[:, cols - STEP : cols].T[STEP - EDGE :]
        inner = pl.ds(0, cols)
        if c == 0:
            corners.append(send(ds.at[pl.ds(EDGE, EDGE), inner], ds.at[pl.ds(EDGE + rows, EDGE), inner], {"lat": up}))
        if c == count - 1:
            corners.append(send(ds.at[pl.ds(rows, EDGE), inner], ds.at[pl.ds(0, EDGE), inner], {"lat": down}))
        for stage, dst, z in ((sd_l, hd_r, left), (sd_r, hd_l, right)):
            mains.append((i, send(stage.at[c], dst.at[c + 1], {"lon": z})))
            if c == 0:
                corners.append(send(stage.at[c], dst.at[count + 1], {"lat": up, "lon": z}))
            if c == count - 1:
                corners.append(send(stage.at[c], dst.at[0], {"lat": down, "lon": z}))

    def side_block(i):
        zeros = jnp.zeros((STEP - 2 * EDGE, PART), F32)
        return jnp.concatenate([hd_r[i, :, 0:PART], zeros, hd_l[i, :, 0:PART]], axis=0).T

    def take(most):
        while mains and mains[0][0] <= most:
            i, copy = mains.pop(0)
            copy.wait_recv()
            if not mains or mains[0][0] != i:
                at = EDGE + parts[i] * PART
                ds[at : at + PART, cols:wide] = side_block(parts[i] + 1)

    def take_corners():
        for copy in corners:
            copy.wait_recv()
        ds[top, cols:wide] = side_block(0)[PART - EDGE :]
        ds[bottom, cols:wide] = side_block(count + 1)[0:EDGE]
        ds[top, :] = jnp.where(lat > 0, ds[top, :], 0.0)
        ds[bottom, :] = jnp.where(lat < n_lat - 1, ds[bottom, :], 0.0)

    def finish(at, n):
        mine = slice(at, at + n)
        o_p[0, mine, :], o_s[0, mine, :] = backward(at, n, held, by_height)

    moving, mains, corners = {}, [], []
    lifted(order[0])
    logs(order[0])
    rest()
    started = 0
    for f in range(1, 3):
        lifted(order[f])
        if bits == 2:
            join(started, 0)
            started += 1
        logs(order[f])
    ready = 3
    if bits != 2:
        for c in order[ready:]:
            lifted(c)
            logs(c)
        for bit in range(bits - 1):
            for i in range(count):
                join(i, bit)
        ready, started = len(order), count
    areas = regions(rows)
    ends = made_by(rows)
    done = 0
    for i in range(count):
        join(i, bits - 1)
        if started < count:
            join(started, 0)
            started += 1
        while ready < len(order) and ends[ready - 1] < i + 5:
            lifted(order[ready])
            logs(order[ready])
            ready += 1
        final = i == count - 1
        if final:
            at, n = areas[done]
            take(i - 1)
            finish(at, n // 2)
        second(i)
        if final:
            finish(at + n // 2, n - n // 2)
            take(i)
            continue
        while done < len(areas) - 2 and ends[max(done, 1)] < i:
            take(i - 1)
            if done == 0:
                take_corners()
            finish(*areas[done])
            done += 1
    for copy in sent:
        copy.wait_send()


def write_out(area, p_ref, s_ref, ds, first, lift, ep, t_pair, t_last, low, high, p_out, s_out, p_last, s_last, done):
    at, n = area
    rows = p_ref.shape[1]
    copies = []

    def write(src, dst):
        copies.append(pltpu.make_async_copy(src, dst, done.at[len(copies)]))
        copies[-1].start()

    for r in (pl.ds(0, at), pl.ds(at + n, rows - at - n)):
        write(p_ref.at[0, r], p_out.at[0, r])
        write(s_ref.at[0, r], s_out.at[0, r])
    refs = (ds, first, lift, ep, t_pair, t_last)
    p_last[...], s_last[...] = backward(at, n, refs, {n: low, n + EDGE: high})
    write(p_last, p_out.at[0, pl.ds(at, n)])
    write(s_last, s_out.at[0, pl.ds(at, n)])
    for copy in copies:
        copy.wait()


def per_device(n_hour, n_lat, n_lon, precip, scaling, hour_weight, cotangent):
    rows, cols = precip.shape[1:]
    tall, wide, lanes = rows + 2 * EDGE, cols + STEP, rows + 2 * STEP
    bits = n_hour.bit_length() - 1
    count = rows // PART
    assert n_hour == 1 << bits and bits > 0 and min(n_lat, n_lon) > 1
    assert rows % STEP == 0 and cols % (2 * STEP) == 0 and rows >= 4 * STEP
    ext, tile = pltpu.VMEM((tall, wide), F32), pltpu.VMEM((rows, cols), F32)
    pair = pltpu.VMEM((2, rows, cols), F32)
    steps = pltpu.VMEM((max(bits - 1, 1), rows, cols), F32)
    copies = 12 + count * (bits + 3) + 6
    out = jax.ShapeDtypeStruct(precip.shape, F32)
    hbm = pl.BlockSpec(memory_space=pl.ANY)
    vmem = pl.BlockSpec(memory_space=pltpu.VMEM)
    held = pltpu.VMEM(precip.shape, F32)
    stage, halo = pltpu.VMEM((EDGE + RADIUS, rows), F32), pltpu.VMEM((EDGE + RADIUS, lanes), F32)
    piece_stage, piece_halo = pltpu.VMEM((count, EDGE, STEP), F32), pltpu.VMEM((count + 2, EDGE, STEP), F32)
    heads = heights(rows)
    fixed = [(8 * STEP, 2 * STEP), (5 * STEP, STEP)] + [(n, 3 * (n + EDGE)) for n in heads]
    held = [pltpu.VMEM(precip.shape, F32)] * 2 + [ext] * 4 + [pltpu.VMEM(k, BF16) for k in fixed]
    size = 4 * (2 * rows * cols + 4 * tall * wide) + sum(2 * k[0] * (-(-k[1] // STEP) * STEP) for k in fixed)
    spare = (64 * 2**20 - size - 2**19) // 1024 * 1024
    made = pl.pallas_call(
        functools.partial(kernel, (n_hour, n_lat, n_lon, rows, cols)),
        out_shape=tuple(held),
        in_specs=[hbm, hbm, pl.BlockSpec(memory_space=pltpu.SMEM), hbm],
        out_specs=tuple([vmem] * len(held)),
        scratch_shapes=[
            ext, tile, pair, tile, steps, steps, pair, tile,
            stage, stage, halo, halo, piece_stage, piece_stage, piece_halo, piece_halo,
            pltpu.SemaphoreType.DMA((7,)),
            pltpu.SemaphoreType.DMA((copies,)), pltpu.SemaphoreType.DMA((copies,)),
        ],
        compiler_params=pltpu.CompilerParams(
            collective_id=0, has_side_effects=True, vmem_limit_bytes=spare
        ),
    )(precip, scaling, hour_weight, cotangent)
    at, n = regions(rows)[-1]
    bands = dict(zip(heads, made[8:]))
    return pl.pallas_call(
        functools.partial(write_out, (at, n)),
        out_shape=(out, out),
        in_specs=[vmem] * 10,
        out_specs=(hbm, hbm),
        scratch_shapes=[
            pltpu.VMEM((n, cols), F32), pltpu.VMEM((n, cols), F32), pltpu.SemaphoreType.DMA((6,)),
        ],
        compiler_params=pltpu.CompilerParams(vmem_limit_bytes=8 * 2**20),
    )(*made[:8], bands[n], bands[n + EDGE])


def solution(mesh):
    field = P("hour", "lat", "lon")
    sizes = [mesh.shape[a] for a in ("hour", "lat", "lon")]
    return jax.shard_map(
        functools.partial(per_device, *sizes), mesh=mesh,
        in_specs=(field, field, P("hour"), field), out_specs=(field, field), check_vma=False,
    )
```

```python
import functools
import math
import jax
import jax.numpy as jnp
from jax import lax
from jax.experimental import pallas as pl
from jax.experimental.pallas import tpu as pltpu
from jax.sharding import PartitionSpec as P

RADIUS = 8
PHI = 0.8
SPREAD = 50.0
STEP = 128
PART = STEP // 2
EDGE = 2 * RADIUS
TOTAL = sum(math.exp(-d * d / SPREAD) for d in range(-RADIUS, RADIUS + 1))
MESH = pl.DeviceIdType.MESH
F32, BF16 = jnp.float32, jnp.bfloat16


def split(x):
    high = x.astype(BF16)
    return high, (x - high.astype(F32)).astype(BF16)


def taps(d):
    d = d.astype(F32)
    return jnp.where(jnp.abs(d) <= RADIUS, jnp.exp(-d * d / SPREAD) / TOTAL, 0.0)


def either(k, low):
    high = k.astype(BF16).astype(F32)
    return jnp.where(low, k - high, high).astype(BF16)


def places(rows, cols):
    return [lax.broadcasted_iota(jnp.int32, (rows, cols), at) for at in (0, 1)]


def stacked_rows(n):
    depth = n + EDGE
    i, j = places(n, 3 * depth)
    third = j >= 2 * depth
    at = jnp.where(third, j - 2 * depth, jnp.where(j >= depth, j - depth, j))
    return either(taps(at - i - RADIUS), third)


def stacked_cols(size):
    i, j = places(size, size)
    high, low = split(taps(i - j))
    i, j = places(2 * STEP, size)
    middle = (i >= STEP + STEP // 4) & (i < STEP + 3 * STEP // 4)
    lane = jnp.where(i >= STEP, i - STEP, i)
    lane = jnp.where(middle, jnp.where(lane >= STEP // 2, lane - STEP // 2, lane + STEP // 2), lane)
    near = taps(jnp.where(lane >= STEP // 2, lane - STEP, lane + size) - j)
    return jnp.concatenate([high, high, low, either(near, middle)], axis=0)


def row_pass(weights, x):
    high, low = split(x)
    return jnp.dot(weights[...], jnp.concatenate([high, low, high], axis=0), preferred_element_type=F32)


def col_pass(pair, last, x, width):
    high, low = split(x)
    blocks = x.shape[1] // STEP
    lane = lax.broadcasted_iota(jnp.int32, (x.shape[0], STEP), 1)
    middle = (lane >= STEP // 4) & (lane < 3 * STEP // 4)
    out = []
    for start in range(0, width, 2 * STEP):
        size = min(2 * STEP, width - start)
        before = (start // STEP - 1) % blocks * STEP
        after = (start + size) // STEP % blocks * STEP
        beside = jnp.where(lane >= STEP // 2, x[:, before : before + STEP], x[:, after : after + STEP])
        near = beside.astype(BF16)
        rounded = near.astype(F32)
        mixed = jnp.where(middle, pltpu.roll(rounded, STEP // 2, 1), beside - rounded).astype(BF16)
        h, l = high[:, start : start + size], low[:, start : start + size]
        weights = pair if size == 2 * STEP else last
        out.append(jnp.dot(
            jnp.concatenate([h, l, h, near, mixed], axis=1), weights[...], preferred_element_type=F32
        ))
    return jnp.concatenate(out, axis=1)


def backward(at, n, refs, bands):
    ds, first, lift, ep, pair, last = refs
    cols = ds.shape[1] - STEP
    span = slice(at + RADIUS, at + n + 3 * RADIUS)
    d = col_pass(pair, last, row_pass(bands[n + EDGE], ds[at : at + n + 2 * EDGE, :]), ds.shape[1])
    carried = PHI * d * lift[span, :]
    out = carried[RADIUS : RADIUS + n, 0:cols] / ep[at + EDGE : at + EDGE + n, 0:cols]
    return out, col_pass(pair, last, row_pass(bands[n], -carried / first[span, :]), cols)


def plan(rows):
    sizes = [STEP // 2] + [STEP] * ((rows - 2 * STEP) // STEP) + [STEP // 2, STEP]
    pieces = [(sum(sizes[:i]), n) for i, n in enumerate(sizes)]
    last = len(pieces) - 1
    return pieces, [0, last] + list(range(1, last))


def split_up(rows):
    pieces, order = plan(rows)
    found = []
    for c in order:
        at, n = pieces[c]
        own = list(range(at // PART, (at + n) // PART))
        found += own[::-1] if c == len(pieces) - 1 else own
    return found


def made_by(rows):
    pieces, order = plan(rows)
    found, at = [], -1
    for c in order:
        at += pieces[c][1] // PART
        found.append(at)
    return found


def heights(rows):
    found = set()
    spans = plan(rows)[0] + regions(rows)
    spans.append((0, spans[-2][1] // 2))
    for _, n in spans:
        found |= {n, n + EDGE}
    return sorted(found)


def regions(rows):
    pieces, order = plan(rows)
    last = len(pieces) - 1
    found = [(0, pieces[0][1] - EDGE), (pieces[last][0] + EDGE, pieces[last][1] - EDGE)]
    at = found[0][1]
    for c in order[2:]:
        end = sum(pieces[c]) + (EDGE if c == last - 1 else -EDGE)
        found.append((at, end - at))
        at = end
    return found


def kernel(sizes, p_hbm, s_hbm, w_ref, c_hbm, *refs):
    heads = heights(sizes[3])
    o_p, o_s, ds, first, lift, ep, *refs = refs
    weights, refs = refs[: 2 + len(heads)], refs[2 + len(heads) :]
    (es, ct, own, got, part, other, both, scale,
     st_l, st_r, h_l, h_r, sd_l, sd_r, hd_l, hd_r, local, sends, recvs) = refs
    t_pair, t_last, *bands = weights
    n_hour, n_lat, n_lon, rows, cols = sizes
    pieces, order = plan(rows)
    parts = split_up(rows)
    count = len(parts)
    by_height = dict(zip(heads, bands))
    held = (ds, first, lift, ep, t_pair, t_last)
    tall, wide = rows + 2 * EDGE, cols + STEP
    bits = n_hour.bit_length() - 1
    hour, lat, lon = (lax.axis_index(a) for a in ("hour", "lat", "lon"))
    side = lax.rem(hour, 2)
    up, down = lax.rem(lat + n_lat - 1, n_lat), lax.rem(lat + 1, n_lat)
    left, right = lax.rem(lon + n_lon - 1, n_lon), lax.rem(lon + 1, n_lon)

    def flip(bit):
        m = 1 << bit
        return hour + m - 2 * m * lax.rem(hour // m, 2)

    own_rows = pl.ds(EDGE, rows)
    loads = []
    for z, n in ((0, STEP), (cols - STEP, STEP), (STEP, cols - 2 * STEP)):
        for src, dst in ((s_hbm, es), (p_hbm, ep)):
            lanes = pl.ds(z, n)
            loads.append(pltpu.make_async_copy(src.at[0, :, lanes], dst.at[own_rows, lanes], local.at[len(loads)]))
    loads.append(pltpu.make_async_copy(c_hbm.at[0], ct, local.at[len(loads)]))
    for copy in loads:
        copy.start()

    barrier = pltpu.get_barrier_semaphore()
    lats = [up, down] if n_lat > 2 else [down]
    lons = [left, right] if n_lon > 2 else [right]
    peers = [{"lon": z} for z in lons] + [{"lat": x} for x in lats]
    peers += [{"lat": x, "lon": z} for x in lats for z in lons]
    peers += [{"hour": flip(bit)} for bit in range(bits)]
    for peer in peers:
        pl.semaphore_signal(barrier, inc=1, device_id=peer, device_id_type=MESH)

    sd_l[...] = jnp.zeros_like(sd_l)
    sd_r[...] = jnp.zeros_like(sd_r)
    pl.semaphore_wait(barrier, len(peers))

    sent = []

    def send(src, dst, peer):
        at = len(sent)
        copy = pltpu.make_async_remote_copy(
            src_ref=src, dst_ref=dst, send_sem=sends.at[at], recv_sem=recvs.at[at],
            device_id=peer, device_id_type=MESH,
        )
        copy.start()
        sent.append(copy)
        return copy

    def fill(at, n):
        r, lanes = slice(EDGE + at, EDGE + at + n), slice(at, at + n)
        st_l[0:EDGE, lanes] = es[r, 0:STEP].T[0:EDGE]
        st_r[0:EDGE, lanes] = es[r, cols - STEP : cols].T[STEP - EDGE :]
        st_l[EDGE:, lanes] = ep[r, 0:STEP].T[0:RADIUS]
        st_r[EDGE:, lanes] = ep[r, cols - STEP : cols].T[STEP - RADIUS :]

    early, late = [], []
    for src, dst in ((s_hbm, es), (p_hbm, ep)):
        early.append(send(src.at[0, pl.ds(rows - EDGE, EDGE)], dst.at[pl.ds(0, EDGE), pl.ds(0, cols)], {"lat": down}))
    for copy in loads[:4]:
        copy.wait()
    fill(0, STEP)
    fill(rows - STEP, STEP)
    first_lanes, last_lanes = pl.ds(0, STEP), pl.ds(rows - STEP, STEP)
    sides = ((st_l, h_r, left), (st_r, h_l, right))
    for stage, dst, z in sides:
        early.append(send(stage.at[:, first_lanes], dst.at[:, pl.ds(STEP, STEP)], {"lon": z}))
        early.append(send(stage.at[:, last_lanes], dst.at[:, first_lanes], {"lat": down, "lon": z}))
    fill(STEP, rows - 2 * STEP)
    for stage, dst, z in sides:
        late.append(send(stage.at[:, first_lanes], dst.at[:, pl.ds(STEP + rows, STEP)], {"lat": up, "lon": z}))
        late.append(send(stage.at[:, pl.ds(STEP, rows - STEP)], dst.at[:, pl.ds(2 * STEP, rows - STEP)], {"lon": z}))
    for src, dst in ((s_hbm, es), (p_hbm, ep)):
        late.append(send(src.at[0, pl.ds(0, EDGE)], dst.at[pl.ds(EDGE + rows, EDGE), pl.ds(0, cols)], {"lat": up}))

    top, bottom = slice(0, EDGE), slice(EDGE + rows, tall)

    def beside(at, n, start, skip, size):
        lanes = slice(at, at + n)
        for dst, low, high in ((es, 0, EDGE), (ep, EDGE, EDGE + RADIUS)):
            ones = jnp.ones((STEP - 2 * (high - low), n), F32)
            block = jnp.concatenate([h_r[low:high, lanes], ones, h_l[low:high, lanes]], axis=0).T
            dst[start : start + size, cols:wide] = block[skip : skip + size]

    weight = w_ref[0]
    t_pair[...] = stacked_cols(2 * STEP)
    t_last[...] = stacked_cols(STEP)
    for n, ref in by_height.items():
        ref[...] = stacked_rows(n)
    for copy in loads[4:]:
        copy.wait()
    for copy in early:
        copy.wait_recv()
    beside(0, 2 * STEP, 0, STEP - EDGE, STEP + EDGE)
    es[top, :] = jnp.where(lat > 0, es[top, :], 0.0)

    def rest():
        for copy in late:
            copy.wait_recv()
        beside(2 * STEP, rows, STEP + EDGE, 0, rows - STEP + EDGE)
        es[bottom, :] = jnp.where(lat < n_lat - 1, es[bottom, :], 0.0)

    def lifted(c):
        at, n = pieces[c]
        span = slice(at + RADIUS, at + RADIUS + n + EDGE)
        a = col_pass(t_pair, t_last, row_pass(by_height[n + EDGE], es[at : at + n + 2 * EDGE, :]), wide)
        first[span, :] = a
        u = jnp.exp(PHI * jnp.log(ep[span, :] / a))
        if c == 0 or c == len(pieces) - 1:
            e = lax.broadcasted_iota(jnp.int32, u.shape, 0) + (at + RADIUS)
            inside = ((lat > 0) | (e >= EDGE)) & ((lat < n_lat - 1) | (e < EDGE + rows))
            u = jnp.where(inside, u, 0.0)
        lift[span, :] = u

    def logs(c):
        at, n = pieces[c]
        b = col_pass(t_pair, t_last, row_pass(by_height[n], lift[at + RADIUS : at + RADIUS + n + EDGE, :]), cols)
        logb = jnp.log(b)
        mine = slice(at, at + n)
        own[0, mine, :] = weight * logb
        own[1, mine, :] = ct[mine, :] * jnp.exp(-PHI * logb)
        scale[mine, :] = PHI / b
        for i, q in enumerate(parts):
            if at <= q * PART < at + n:
                r = pl.ds(q * PART, PART)
                moving[i] = send(own.at[1 - side, r], got.at[r], {"hour": flip(0)})

    def join(i, bit):
        moving[i].wait_recv()
        at = parts[i] * PART
        mine = slice(at, at + PART)
        r = pl.ds(at, PART)
        if bit == 0:
            value = own[side, mine, :] + got[mine, :]
        else:
            value = part[bit - 1, mine, :] + other[bit - 1, mine, :]
        if bit == bits - 1:
            both[side, mine, :] = value
            moving[i] = send(both.at[side, r], both.at[side, r], {"hour": flip(0)})
            return
        part[bit, mine, :] = value
        moving[i] = send(part.at[bit, r], other.at[bit, r], {"hour": flip(bit + 1)})

    def second(i):
        moving[i].wait_recv()
        c = parts[i]
        at, n = c * PART, PART
        mine = slice(at, at + n)
        d = jnp.exp(PHI * both[0, mine, :]) * (weight * both[1, mine, :] - own[1, mine, :]) * scale[mine, :]
        ds[at + EDGE : at + EDGE + n, 0:cols] = d
        sd_l[c, :, 0:n] = d[:, 0:STEP].T[0:EDGE]
        sd_r[c, :, 0:n] = d[:, cols - STEP : cols].T[STEP - EDGE :]
        inner = pl.ds(0, cols)
        if c == 0:
            corners.append(send(ds.at[pl.ds(EDGE, EDGE), inner], ds.at[pl.ds(EDGE + rows, EDGE), inner], {"lat": up}))
        if c == count - 1:
            corners.append(send(ds.at[pl.ds(rows, EDGE), inner], ds.at[pl.ds(0, EDGE), inner], {"lat": down}))
        for stage, dst, z in ((sd_l, hd_r, left), (sd_r, hd_l, right)):
            mains.append((i, send(stage.at[c], dst.at[c + 1], {"lon": z})))
            if c == 0:
                corners.append(send(stage.at[c], dst.at[count + 1], {"lat": up, "lon": z}))
            if c == count - 1:
                corners.append(send(stage.at[c], dst.at[0], {"lat": down, "lon": z}))

    def side_block(i):
        zeros = jnp.zeros((STEP - 2 * EDGE, PART), F32)
        return jnp.concatenate([hd_r[i, :, 0:PART], zeros, hd_l[i, :, 0:PART]], axis=0).T

    def take(most):
        while mains and mains[0][0] <= most:
            i, copy = mains.pop(0)
            copy.wait_recv()
            if not mains or mains[0][0] != i:
                at = EDGE + parts[i] * PART
                ds[at : at + PART, cols:wide] = side_block(parts[i] + 1)

    def take_corners():
        for copy in corners:
            copy.wait_recv()
        ds[top, cols:wide] = side_block(0)[PART - EDGE :]
        ds[bottom, cols:wide] = side_block(count + 1)[0:EDGE]
        ds[top, :] = jnp.where(lat > 0, ds[top, :], 0.0)
        ds[bottom, :] = jnp.where(lat < n_lat - 1, ds[bottom, :], 0.0)

    def finish(at, n):
        mine = slice(at, at + n)
        o_p[0, mine, :], o_s[0, mine, :] = backward(at, n, held, by_height)

    moving, mains, corners = {}, [], []
    lifted(order[0])
    logs(order[0])
    rest()
    started = 0
    for f in range(1, 3):
        lifted(order[f])
        if bits == 2:
            join(started, 0)
            started += 1
        logs(order[f])
    ready = 3
    if bits == 2:
        join(started, 0)
        started += 1
    else:
        for c in order[ready:]:
            lifted(c)
            logs(c)
        for bit in range(bits - 1):
            for i in range(count):
                join(i, bit)
        ready, started = len(order), count
    areas = regions(rows)
    ends = made_by(rows)
    done = 0
    for i in range(count):
        join(i, bits - 1)
        if started < count:
            join(started, 0)
            started += 1
        if 0 < i < count - 1:
            second(i - 1)
        while ready < len(order) and ends[ready - 1] < i + 5:
            lifted(order[ready])
            logs(order[ready])
            ready += 1
        if i == count - 1:
            at, n = areas[done]
            take(i - 1)
            finish(at, n // 2)
            second(i)
            finish(at + n // 2, n - n // 2)
            take(i)
            break
        while done < len(areas) - 2 and ends[max(done, 1)] < i - 1:
            take(i - 2)
            if done == 0:
                take_corners()
            finish(*areas[done])
            done += 1
            if i < count - 2:
                break
        if i == count - 2:
            second(i)
    for copy in sent:
        copy.wait_send()


def write_out(area, p_ref, s_ref, ds, first, lift, ep, t_pair, t_last, low, high, p_out, s_out, p_last, s_last, done):
    at, n = area
    rows = p_ref.shape[1]
    copies = []

    def write(src, dst):
        copies.append(pltpu.make_async_copy(src, dst, done.at[len(copies)]))
        copies[-1].start()

    for r in (pl.ds(0, at), pl.ds(at + n, rows - at - n)):
        write(p_ref.at[0, r], p_out.at[0, r])
        write(s_ref.at[0, r], s_out.at[0, r])
    refs = (ds, first, lift, ep, t_pair, t_last)
    p_last[...], s_last[...] = backward(at, n, refs, {n: low, n + EDGE: high})
    write(p_last, p_out.at[0, pl.ds(at, n)])
    write(s_last, s_out.at[0, pl.ds(at, n)])
    for copy in copies:
        copy.wait()


def per_device(n_hour, n_lat, n_lon, precip, scaling, hour_weight, cotangent):
    rows, cols = precip.shape[1:]
    tall, wide, lanes = rows + 2 * EDGE, cols + STEP, rows + 2 * STEP
    bits = n_hour.bit_length() - 1
    count = rows // PART
    assert n_hour == 1 << bits and bits > 0 and min(n_lat, n_lon) > 1
    assert rows % STEP == 0 and cols % (2 * STEP) == 0 and rows >= 4 * STEP
    ext, tile = pltpu.VMEM((tall, wide), F32), pltpu.VMEM((rows, cols), F32)
    pair = pltpu.VMEM((2, rows, cols), F32)
    steps = pltpu.VMEM((max(bits - 1, 1), rows, cols), F32)
    copies = 12 + count * (bits + 3) + 6
    out = jax.ShapeDtypeStruct(precip.shape, F32)
    hbm = pl.BlockSpec(memory_space=pl.ANY)
    vmem = pl.BlockSpec(memory_space=pltpu.VMEM)
    held = pltpu.VMEM(precip.shape, F32)
    stage, halo = pltpu.VMEM((EDGE + RADIUS, rows), F32), pltpu.VMEM((EDGE + RADIUS, lanes), F32)
    piece_stage, piece_halo = pltpu.VMEM((count, EDGE, STEP), F32), pltpu.VMEM((count + 2, EDGE, STEP), F32)
    heads = heights(rows)
    fixed = [(8 * STEP, 2 * STEP), (5 * STEP, STEP)] + [(n, 3 * (n + EDGE)) for n in heads]
    held = [pltpu.VMEM(precip.shape, F32)] * 2 + [ext] * 4 + [pltpu.VMEM(k, BF16) for k in fixed]
    size = 4 * (2 * rows * cols + 4 * tall * wide) + sum(2 * k[0] * (-(-k[1] // STEP) * STEP) for k in fixed)
    spare = (64 * 2**20 - size - 2**19) // 1024 * 1024
    made = pl.pallas_call(
        functools.partial(kernel, (n_hour, n_lat, n_lon, rows, cols)),
        out_shape=tuple(held),
        in_specs=[hbm, hbm, pl.BlockSpec(memory_space=pltpu.SMEM), hbm],
        out_specs=tuple([vmem] * len(held)),
        scratch_shapes=[
            ext, tile, pair, tile, steps, steps, pair, tile,
            stage, stage, halo, halo, piece_stage, piece_stage, piece_halo, piece_halo,
            pltpu.SemaphoreType.DMA((7,)),
            pltpu.SemaphoreType.DMA((copies,)), pltpu.SemaphoreType.DMA((copies,)),
        ],
        compiler_params=pltpu.CompilerParams(
            collective_id=0, has_side_effects=True, vmem_limit_bytes=spare
        ),
    )(precip, scaling, hour_weight, cotangent)
    at, n = regions(rows)[-1]
    bands = dict(zip(heads, made[8:]))
    return pl.pallas_call(
        functools.partial(write_out, (at, n)),
        out_shape=(out, out),
        in_specs=[vmem] * 10,
        out_specs=(hbm, hbm),
        scratch_shapes=[
            pltpu.VMEM((n, cols), F32), pltpu.VMEM((n, cols), F32), pltpu.SemaphoreType.DMA((6,)),
        ],
        compiler_params=pltpu.CompilerParams(vmem_limit_bytes=8 * 2**20),
    )(*made[:8], bands[n], bands[n + EDGE])


def solution(mesh):
    field = P("hour", "lat", "lon")
    sizes = [mesh.shape[a] for a in ("hour", "lat", "lon")]
    return jax.shard_map(
        functools.partial(per_device, *sizes), mesh=mesh,
        in_specs=(field, field, P("hour"), field), out_specs=(field, field), check_vma=False,
    )
```

```python
import functools
import math
import jax
import jax.numpy as jnp
from jax import lax
from jax.experimental import pallas as pl
from jax.experimental.pallas import tpu as pltpu
from jax.sharding import PartitionSpec as P

RADIUS = 8
PHI = 0.8
SPREAD = 50.0
STEP = 128
EDGE = 2 * RADIUS
TOTAL = sum(math.exp(-d * d / SPREAD) for d in range(-RADIUS, RADIUS + 1))
MESH = pl.DeviceIdType.MESH
F32, BF16 = jnp.float32, jnp.bfloat16


def split(x):
    high = x.astype(BF16)
    return high, (x - high.astype(F32)).astype(BF16)


def taps(d):
    d = d.astype(F32)
    return jnp.where(jnp.abs(d) <= RADIUS, jnp.exp(-d * d / SPREAD) / TOTAL, 0.0)


def either(k, low):
    high = k.astype(BF16).astype(F32)
    return jnp.where(low, k - high, high).astype(BF16)


def places(rows, cols):
    return [lax.broadcasted_iota(jnp.int32, (rows, cols), at) for at in (0, 1)]


def stacked_rows(n):
    depth = n + EDGE
    i, j = places(n, 3 * depth)
    third = j >= 2 * depth
    at = jnp.where(third, j - 2 * depth, jnp.where(j >= depth, j - depth, j))
    return either(taps(at - i - RADIUS), third)


def stacked_cols(size):
    i, j = places(size, size)
    high, low = split(taps(i - j))
    i, j = places(2 * STEP, size)
    middle = (i >= STEP + STEP // 4) & (i < STEP + 3 * STEP // 4)
    lane = jnp.where(i >= STEP, i - STEP, i)
    lane = jnp.where(middle, jnp.where(lane >= STEP // 2, lane - STEP // 2, lane + STEP // 2), lane)
    near = taps(jnp.where(lane >= STEP // 2, lane - STEP, lane + size) - j)
    return jnp.concatenate([high, high, low, either(near, middle)], axis=0)


def row_pass(weights, x):
    high, low = split(x)
    return jnp.dot(weights[...], jnp.concatenate([high, low, high], axis=0), preferred_element_type=F32)


def col_pass(pair, last, x, width):
    high, low = split(x)
    blocks = x.shape[1] // STEP
    lane = lax.broadcasted_iota(jnp.int32, (x.shape[0], STEP), 1)
    middle = (lane >= STEP // 4) & (lane < 3 * STEP // 4)
    out = []
    for start in range(0, width, 2 * STEP):
        size = min(2 * STEP, width - start)
        before = (start // STEP - 1) % blocks * STEP
        after = (start + size) // STEP % blocks * STEP
        beside = jnp.where(lane >= STEP // 2, x[:, before : before + STEP], x[:, after : after + STEP])
        near = beside.astype(BF16)
        rounded = near.astype(F32)
        mixed = jnp.where(middle, pltpu.roll(rounded, STEP // 2, 1), beside - rounded).astype(BF16)
        h, l = high[:, start : start + size], low[:, start : start + size]
        weights = pair if size == 2 * STEP else last
        out.append(jnp.dot(
            jnp.concatenate([h, l, h, near, mixed], axis=1), weights[...], preferred_element_type=F32
        ))
    return jnp.concatenate(out, axis=1)


def backward(at, n, refs, bands):
    ds, first, lift, ep, pair, last = refs
    cols = ds.shape[1] - STEP
    span = slice(at + RADIUS, at + n + 3 * RADIUS)
    d = col_pass(pair, last, row_pass(bands[n + EDGE], ds[at : at + n + 2 * EDGE, :]), ds.shape[1])
    carried = PHI * d * lift[span, :]
    out = carried[RADIUS : RADIUS + n, 0:cols] / ep[at + EDGE : at + EDGE + n, 0:cols]
    return out, col_pass(pair, last, row_pass(bands[n], -carried / first[span, :]), cols)


def plan(rows):
    sizes = [STEP // 2] + [STEP] * ((rows - 2 * STEP) // STEP) + [STEP // 2, STEP]
    pieces = [(sum(sizes[:i]), n) for i, n in enumerate(sizes)]
    last = len(pieces) - 1
    return pieces, [0, last] + list(range(1, last))


def heights(rows):
    found = set()
    pieces, _ = plan(rows)
    for _, n in pieces:
        found |= {n, n + EDGE}
    areas = regions(rows)
    areas.append((0, areas[-2][1] // 2))
    for _, n in areas:
        found |= {n, n + EDGE}
    return sorted(found)


def regions(rows):
    pieces, order = plan(rows)
    last = len(pieces) - 1
    found = [(0, pieces[0][1] - EDGE), (pieces[last][0] + EDGE, pieces[last][1] - EDGE)]
    at = found[0][1]
    for c in order[2:]:
        end = sum(pieces[c]) + (EDGE if c == last - 1 else -EDGE)
        found.append((at, end - at))
        at = end
    return found


def kernel(sizes, p_hbm, s_hbm, w_ref, c_hbm, *refs):
    heads = heights(sizes[3])
    o_p, o_s, ds, first, lift, ep, *refs = refs
    weights, refs = refs[: 2 + len(heads)], refs[2 + len(heads) :]
    (es, ct, own, got, part, other, both, scale,
     st_l, st_r, h_l, h_r, sd_l, sd_r, hd_l, hd_r, local, sends, recvs) = refs
    t_pair, t_last, *bands = weights
    n_hour, n_lat, n_lon, rows, cols = sizes
    pieces, order = plan(rows)
    count = len(pieces)
    by_height = dict(zip(heads, bands))
    held = (ds, first, lift, ep, t_pair, t_last)
    tall, wide = rows + 2 * EDGE, cols + STEP
    bits = n_hour.bit_length() - 1
    hour, lat, lon = (lax.axis_index(a) for a in ("hour", "lat", "lon"))
    side = lax.rem(hour, 2)
    up, down = lax.rem(lat + n_lat - 1, n_lat), lax.rem(lat + 1, n_lat)
    left, right = lax.rem(lon + n_lon - 1, n_lon), lax.rem(lon + 1, n_lon)

    def flip(bit):
        m = 1 << bit
        return hour + m - 2 * m * lax.rem(hour // m, 2)

    own_rows = pl.ds(EDGE, rows)
    loads = []
    for z, n in ((0, STEP), (cols - STEP, STEP), (STEP, cols - 2 * STEP)):
        for src, dst in ((s_hbm, es), (p_hbm, ep)):
            lanes = pl.ds(z, n)
            loads.append(pltpu.make_async_copy(src.at[0, :, lanes], dst.at[own_rows, lanes], local.at[len(loads)]))
    loads.append(pltpu.make_async_copy(c_hbm.at[0], ct, local.at[len(loads)]))
    for copy in loads:
        copy.start()

    barrier = pltpu.get_barrier_semaphore()
    lats = [up, down] if n_lat > 2 else [down]
    lons = [left, right] if n_lon > 2 else [right]
    peers = [{"lon": z} for z in lons] + [{"lat": x} for x in lats]
    peers += [{"lat": x, "lon": z} for x in lats for z in lons]
    peers += [{"hour": flip(bit)} for bit in range(bits)]
    for peer in peers:
        pl.semaphore_signal(barrier, inc=1, device_id=peer, device_id_type=MESH)

    sd_l[...] = jnp.zeros_like(sd_l)
    sd_r[...] = jnp.zeros_like(sd_r)
    pl.semaphore_wait(barrier, len(peers))

    sent = []

    def send(src, dst, peer):
        at = len(sent)
        copy = pltpu.make_async_remote_copy(
            src_ref=src, dst_ref=dst, send_sem=sends.at[at], recv_sem=recvs.at[at],
            device_id=peer, device_id_type=MESH,
        )
        copy.start()
        sent.append(copy)
        return copy

    def fill(at, n):
        r, lanes = slice(EDGE + at, EDGE + at + n), slice(at, at + n)
        st_l[0:EDGE, lanes] = es[r, 0:STEP].T[0:EDGE]
        st_r[0:EDGE, lanes] = es[r, cols - STEP : cols].T[STEP - EDGE :]
        st_l[EDGE:, lanes] = ep[r, 0:STEP].T[0:RADIUS]
        st_r[EDGE:, lanes] = ep[r, cols - STEP : cols].T[STEP - RADIUS :]

    early, late = [], []
    for src, dst in ((s_hbm, es), (p_hbm, ep)):
        early.append(send(src.at[0, pl.ds(rows - EDGE, EDGE)], dst.at[pl.ds(0, EDGE), pl.ds(0, cols)], {"lat": down}))
    for copy in loads[:4]:
        copy.wait()
    fill(0, STEP)
    fill(rows - STEP, STEP)
    first_lanes, last_lanes = pl.ds(0, STEP), pl.ds(rows - STEP, STEP)
    sides = ((st_l, h_r, left), (st_r, h_l, right))
    for stage, dst, z in sides:
        early.append(send(stage.at[:, first_lanes], dst.at[:, pl.ds(STEP, STEP)], {"lon": z}))
        early.append(send(stage.at[:, last_lanes], dst.at[:, first_lanes], {"lat": down, "lon": z}))
    fill(STEP, rows - 2 * STEP)
    for stage, dst, z in sides:
        late.append(send(stage.at[:, first_lanes], dst.at[:, pl.ds(STEP + rows, STEP)], {"lat": up, "lon": z}))
        late.append(send(stage.at[:, pl.ds(STEP, rows - STEP)], dst.at[:, pl.ds(2 * STEP, rows - STEP)], {"lon": z}))
    for src, dst in ((s_hbm, es), (p_hbm, ep)):
        late.append(send(src.at[0, pl.ds(0, EDGE)], dst.at[pl.ds(EDGE + rows, EDGE), pl.ds(0, cols)], {"lat": up}))

    top, bottom = slice(0, EDGE), slice(EDGE + rows, tall)

    def beside(at, n, start, skip, size):
        lanes = slice(at, at + n)
        for dst, low, high in ((es, 0, EDGE), (ep, EDGE, EDGE + RADIUS)):
            ones = jnp.ones((STEP - 2 * (high - low), n), F32)
            block = jnp.concatenate([h_r[low:high, lanes], ones, h_l[low:high, lanes]], axis=0).T
            dst[start : start + size, cols:wide] = block[skip : skip + size]

    weight = w_ref[0]
    t_pair[...] = stacked_cols(2 * STEP)
    t_last[...] = stacked_cols(STEP)
    for n, ref in by_height.items():
        ref[...] = stacked_rows(n)
    for copy in loads[4:]:
        copy.wait()
    for copy in early:
        copy.wait_recv()
    beside(0, 2 * STEP, 0, STEP - EDGE, STEP + EDGE)
    es[top, :] = jnp.where(lat > 0, es[top, :], 0.0)

    def rest():
        for copy in late:
            copy.wait_recv()
        beside(2 * STEP, rows, STEP + EDGE, 0, rows - STEP + EDGE)
        es[bottom, :] = jnp.where(lat < n_lat - 1, es[bottom, :], 0.0)

    def lifted(c):
        at, n = pieces[c]
        span = slice(at + RADIUS, at + RADIUS + n + EDGE)
        a = col_pass(t_pair, t_last, row_pass(by_height[n + EDGE], es[at : at + n + 2 * EDGE, :]), wide)
        first[span, :] = a
        u = jnp.exp(PHI * jnp.log(ep[span, :] / a))
        if c == 0 or c == count - 1:
            e = lax.broadcasted_iota(jnp.int32, u.shape, 0) + (at + RADIUS)
            inside = ((lat > 0) | (e >= EDGE)) & ((lat < n_lat - 1) | (e < EDGE + rows))
            u = jnp.where(inside, u, 0.0)
        lift[span, :] = u

    def logs(c):
        at, n = pieces[c]
        b = col_pass(t_pair, t_last, row_pass(by_height[n], lift[at + RADIUS : at + RADIUS + n + EDGE, :]), cols)
        logb = jnp.log(b)
        mine = slice(at, at + n)
        own[0, mine, :] = weight * logb
        own[1, mine, :] = ct[mine, :] * jnp.exp(-PHI * logb)
        scale[mine, :] = PHI / b
        r = pl.ds(at, n)
        return send(own.at[1 - side, r], got.at[r], {"hour": flip(0)})

    def join(c, bit, copy):
        copy.wait_recv()
        at, n = pieces[c]
        mine = slice(at, at + n)
        r = pl.ds(at, n)
        if bit == 0:
            value = own[side, mine, :] + got[mine, :]
        else:
            value = part[bit - 1, mine, :] + other[bit - 1, mine, :]
        if bit == bits - 1:
            both[side, mine, :] = value
            return send(both.at[side, r], both.at[side, r], {"hour": flip(0)})
        part[bit, mine, :] = value
        return send(part.at[bit, r], other.at[bit, r], {"hour": flip(bit + 1)})

    def second(c, copy):
        copy.wait_recv()
        at, n = pieces[c]
        mine = slice(at, at + n)
        d = jnp.exp(PHI * both[0, mine, :]) * (weight * both[1, mine, :] - own[1, mine, :]) * scale[mine, :]
        ds[at + EDGE : at + EDGE + n, 0:cols] = d
        sd_l[c, :, 0:n] = d[:, 0:STEP].T[0:EDGE]
        sd_r[c, :, 0:n] = d[:, cols - STEP : cols].T[STEP - EDGE :]
        main, corner = [], []
        inner = pl.ds(0, cols)
        if c == 0:
            corner.append(send(ds.at[pl.ds(EDGE, EDGE), inner], ds.at[pl.ds(EDGE + rows, EDGE), inner], {"lat": up}))
        if c == count - 1:
            corner.append(send(ds.at[pl.ds(rows, EDGE), inner], ds.at[pl.ds(0, EDGE), inner], {"lat": down}))
        for stage, dst, z in ((sd_l, hd_r, left), (sd_r, hd_l, right)):
            main.append(send(stage.at[c], dst.at[c + 1], {"lon": z}))
            if c == 0:
                corner.append(send(stage.at[c], dst.at[count + 1], {"lat": up, "lon": z}))
            if c == count - 1:
                corner.append(send(stage.at[c], dst.at[0], {"lat": down, "lon": z}))
        return main, corner

    def side_block(i, n):
        zeros = jnp.zeros((STEP - 2 * EDGE, n), F32)
        return jnp.concatenate([hd_r[i, :, 0:n], zeros, hd_l[i, :, 0:n]], axis=0).T

    def take_main(c, copies):
        for copy in copies:
            copy.wait_recv()
        at, n = pieces[c]
        ds[EDGE + at : EDGE + at + n, cols:wide] = side_block(c + 1, n)

    def take_corners(copies):
        for copy in copies:
            copy.wait_recv()
        n = pieces[count - 1][1]
        ds[top, cols:wide] = side_block(0, n)[n - EDGE :]
        ds[bottom, cols:wide] = side_block(count + 1, pieces[0][1])[0:EDGE]
        ds[top, :] = jnp.where(lat > 0, ds[top, :], 0.0)
        ds[bottom, :] = jnp.where(lat < n_lat - 1, ds[bottom, :], 0.0)

    def finish(at, n):
        mine = slice(at, at + n)
        o_p[0, mine, :], o_s[0, mine, :] = backward(at, n, held, by_height)

    moving = {}
    joined = 0
    ahead = 3 if bits == 2 else count
    for i, c in enumerate(order):
        lifted(c)
        if 0 < i <= ahead:
            moving[order[i - 1]] = join(order[i - 1], 0, moving[order[i - 1]])
            joined = i
        moving[c] = logs(c)
        if i == 0:
            rest()
    if joined < ahead:
        for c in order[joined:]:
            moving[c] = join(c, 0, moving[c])
        joined = count
    for bit in range(1, bits - 1):
        for c in order:
            moving[c] = join(c, bit, moving[c])
    areas = regions(rows)
    mains, corners = {}, []
    for i, c in enumerate(order):
        if bits > 1:
            moving[c] = join(c, bits - 1, moving[c])
        if joined < count:
            moving[order[joined]] = join(order[joined], 0, moving[order[joined]])
            joined += 1
        final = i == count - 1
        if final:
            at, n = areas[i - 1]
            take_main(order[i - 1], mains[order[i - 1]])
            finish(at, n // 2)
        mains[c], corner = second(c, moving[c])
        corners += corner
        if final:
            finish(at + n // 2, n - n // 2)
        if i == 1:
            take_main(order[0], mains[order[0]])
            take_main(order[1], mains[order[1]])
            take_corners(corners)
            finish(*areas[0])
            finish(*areas[1])
        if 1 < i < count - 2:
            take_main(c, mains[c])
            finish(*areas[i])
    take_main(order[-1], mains[order[-1]])
    for copy in sent:
        copy.wait_send()


def write_out(area, p_ref, s_ref, ds, first, lift, ep, t_pair, t_last, low, high, p_out, s_out, p_last, s_last, done):
    at, n = area
    rows = p_ref.shape[1]
    copies = []

    def write(src, dst):
        copies.append(pltpu.make_async_copy(src, dst, done.at[len(copies)]))
        copies[-1].start()

    for r in (pl.ds(0, at), pl.ds(at + n, rows - at - n)):
        write(p_ref.at[0, r], p_out.at[0, r])
        write(s_ref.at[0, r], s_out.at[0, r])
    refs = (ds, first, lift, ep, t_pair, t_last)
    p_last[...], s_last[...] = backward(at, n, refs, {n: low, n + EDGE: high})
    write(p_last, p_out.at[0, pl.ds(at, n)])
    write(s_last, s_out.at[0, pl.ds(at, n)])
    for copy in copies:
        copy.wait()


def per_device(n_hour, n_lat, n_lon, precip, scaling, hour_weight, cotangent):
    rows, cols = precip.shape[1:]
    tall, wide, lanes = rows + 2 * EDGE, cols + STEP, rows + 2 * STEP
    bits = n_hour.bit_length() - 1
    pieces, _ = plan(rows)
    count = len(pieces)
    assert n_hour == 1 << bits and bits > 0 and min(n_lat, n_lon) > 1
    assert rows % STEP == 0 and cols % (2 * STEP) == 0 and count > 3
    ext, tile = pltpu.VMEM((tall, wide), F32), pltpu.VMEM((rows, cols), F32)
    pair = pltpu.VMEM((2, rows, cols), F32)
    steps = pltpu.VMEM((max(bits - 1, 1), rows, cols), F32)
    copies = 12 + count * (bits + 3) + 6
    out = jax.ShapeDtypeStruct(precip.shape, F32)
    hbm = pl.BlockSpec(memory_space=pl.ANY)
    vmem = pl.BlockSpec(memory_space=pltpu.VMEM)
    held = pltpu.VMEM(precip.shape, F32)
    stage, halo = pltpu.VMEM((EDGE + RADIUS, rows), F32), pltpu.VMEM((EDGE + RADIUS, lanes), F32)
    piece_stage, piece_halo = pltpu.VMEM((count, EDGE, STEP), F32), pltpu.VMEM((count + 2, EDGE, STEP), F32)
    heads = heights(rows)
    fixed = [(8 * STEP, 2 * STEP), (5 * STEP, STEP)] + [(n, 3 * (n + EDGE)) for n in heads]
    held = [pltpu.VMEM(precip.shape, F32)] * 2 + [ext] * 4 + [pltpu.VMEM(k, BF16) for k in fixed]
    size = 4 * (2 * rows * cols + 4 * tall * wide) + sum(2 * k[0] * (-(-k[1] // STEP) * STEP) for k in fixed)
    spare = (64 * 2**20 - size - 2**19) // 1024 * 1024
    made = pl.pallas_call(
        functools.partial(kernel, (n_hour, n_lat, n_lon, rows, cols)),
        out_shape=tuple(held),
        in_specs=[hbm, hbm, pl.BlockSpec(memory_space=pltpu.SMEM), hbm],
        out_specs=tuple([vmem] * len(held)),
        scratch_shapes=[
            ext, tile, pair, tile, steps, steps, pair, tile,
            stage, stage, halo, halo, piece_stage, piece_stage, piece_halo, piece_halo,
            pltpu.SemaphoreType.DMA((7,)),
            pltpu.SemaphoreType.DMA((copies,)), pltpu.SemaphoreType.DMA((copies,)),
        ],
        compiler_params=pltpu.CompilerParams(
            collective_id=0, has_side_effects=True, vmem_limit_bytes=spare
        ),
    )(precip, scaling, hour_weight, cotangent)
    at, n = regions(rows)[-1]
    bands = dict(zip(heads, made[8:]))
    return pl.pallas_call(
        functools.partial(write_out, (at, n)),
        out_shape=(out, out),
        in_specs=[vmem] * 10,
        out_specs=(hbm, hbm),
        scratch_shapes=[
            pltpu.VMEM((n, cols), F32), pltpu.VMEM((n, cols), F32), pltpu.SemaphoreType.DMA((6,)),
        ],
        compiler_params=pltpu.CompilerParams(vmem_limit_bytes=8 * 2**20),
    )(*made[:8], bands[n], bands[n + EDGE])


def solution(mesh):
    field = P("hour", "lat", "lon")
    sizes = [mesh.shape[a] for a in ("hour", "lat", "lon")]
    return jax.shard_map(
        functools.partial(per_device, *sizes), mesh=mesh,
        in_specs=(field, field, P("hour"), field), out_specs=(field, field), check_vma=False,
    )
```

```python
import functools
import math
import jax
import jax.numpy as jnp
from jax import lax
from jax.experimental import pallas as pl
from jax.experimental.pallas import tpu as pltpu
from jax.sharding import PartitionSpec as P

RADIUS = 8
PHI = 0.8
SPREAD = 50.0
STEP = 128
EDGE = 2 * RADIUS
TOTAL = sum(math.exp(-d * d / SPREAD) for d in range(-RADIUS, RADIUS + 1))
MESH = pl.DeviceIdType.MESH
F32, BF16 = jnp.float32, jnp.bfloat16


def split(x):
    high = x.astype(BF16)
    return high, (x - high.astype(F32)).astype(BF16)


def taps(d):
    d = d.astype(F32)
    return jnp.where(jnp.abs(d) <= RADIUS, jnp.exp(-d * d / SPREAD) / TOTAL, 0.0)


def either(k, low):
    high = k.astype(BF16).astype(F32)
    return jnp.where(low, k - high, high).astype(BF16)


def places(rows, cols):
    return [lax.broadcasted_iota(jnp.int32, (rows, cols), at) for at in (0, 1)]


def stacked_rows(n):
    depth = n + EDGE
    i, j = places(n, 3 * depth)
    third = j >= 2 * depth
    at = jnp.where(third, j - 2 * depth, jnp.where(j >= depth, j - depth, j))
    return either(taps(at - i - RADIUS), third)


def stacked_cols(size):
    i, j = places(size, size)
    high, low = split(taps(i - j))
    i, j = places(2 * STEP, size)
    middle = (i >= STEP + STEP // 4) & (i < STEP + 3 * STEP // 4)
    lane = jnp.where(i >= STEP, i - STEP, i)
    lane = jnp.where(middle, jnp.where(lane >= STEP // 2, lane - STEP // 2, lane + STEP // 2), lane)
    near = taps(jnp.where(lane >= STEP // 2, lane - STEP, lane + size) - j)
    return jnp.concatenate([high, high, low, either(near, middle)], axis=0)


def row_pass(weights, x):
    high, low = split(x)
    return jnp.dot(weights[...], jnp.concatenate([high, low, high], axis=0), preferred_element_type=F32)


def col_pass(pair, last, x, width):
    high, low = split(x)
    blocks = x.shape[1] // STEP
    lane = lax.broadcasted_iota(jnp.int32, (x.shape[0], STEP), 1)
    middle = (lane >= STEP // 4) & (lane < 3 * STEP // 4)
    out = []
    for start in range(0, width, 2 * STEP):
        size = min(2 * STEP, width - start)
        before = (start // STEP - 1) % blocks * STEP
        after = (start + size) // STEP % blocks * STEP
        beside = jnp.where(lane >= STEP // 2, x[:, before : before + STEP], x[:, after : after + STEP])
        near = beside.astype(BF16)
        rounded = near.astype(F32)
        mixed = jnp.where(middle, pltpu.roll(rounded, STEP // 2, 1), beside - rounded).astype(BF16)
        h, l = high[:, start : start + size], low[:, start : start + size]
        weights = pair if size == 2 * STEP else last
        out.append(jnp.dot(
            jnp.concatenate([h, l, h, near, mixed], axis=1), weights[...], preferred_element_type=F32
        ))
    return jnp.concatenate(out, axis=1)


def backward(at, n, refs, bands):
    ds, first, lift, ep, pair, last = refs
    cols = ds.shape[1] - STEP
    span = slice(at + RADIUS, at + n + 3 * RADIUS)
    d = col_pass(pair, last, row_pass(bands[n + EDGE], ds[at : at + n + 2 * EDGE, :]), ds.shape[1])
    carried = PHI * d * lift[span, :]
    out = carried[RADIUS : RADIUS + n, 0:cols] / ep[at + EDGE : at + EDGE + n, 0:cols]
    return out, col_pass(pair, last, row_pass(bands[n], -carried / first[span, :]), cols)


def plan(rows):
    sizes = [STEP // 2] + [STEP] * ((rows - 2 * STEP) // STEP) + [STEP // 2, STEP]
    pieces = [(sum(sizes[:i]), n) for i, n in enumerate(sizes)]
    last = len(pieces) - 1
    return pieces, [0, last] + list(range(1, last))


def heights(rows):
    found = set()
    pieces, _ = plan(rows)
    for _, n in pieces:
        found |= {n, n + EDGE}
    for _, n in regions(rows):
        found |= {n, n + EDGE}
    return sorted(found)


def regions(rows):
    pieces, order = plan(rows)
    last = len(pieces) - 1
    found = [(0, pieces[0][1] - EDGE), (pieces[last][0] + EDGE, pieces[last][1] - EDGE)]
    at = found[0][1]
    for c in order[2:]:
        end = sum(pieces[c]) + (EDGE if c == last - 1 else -EDGE)
        found.append((at, end - at))
        at = end
    return found


def kernel(sizes, p_hbm, s_hbm, w_ref, c_hbm, *refs):
    heads = heights(sizes[3])
    o_p, o_s, ds, first, lift, ep, *refs = refs
    weights, refs = refs[: 2 + len(heads)], refs[2 + len(heads) :]
    (es, ct, own, got, part, other, both, scale,
     st_l, st_r, h_l, h_r, sd_l, sd_r, hd_l, hd_r, local, sends, recvs) = refs
    t_pair, t_last, *bands = weights
    n_hour, n_lat, n_lon, rows, cols = sizes
    pieces, order = plan(rows)
    count = len(pieces)
    by_height = dict(zip(heads, bands))
    held = (ds, first, lift, ep, t_pair, t_last)
    tall, wide = rows + 2 * EDGE, cols + STEP
    bits = n_hour.bit_length() - 1
    hour, lat, lon = (lax.axis_index(a) for a in ("hour", "lat", "lon"))
    side = lax.rem(hour, 2)
    up, down = lax.rem(lat + n_lat - 1, n_lat), lax.rem(lat + 1, n_lat)
    left, right = lax.rem(lon + n_lon - 1, n_lon), lax.rem(lon + 1, n_lon)

    def flip(bit):
        m = 1 << bit
        return hour + m - 2 * m * lax.rem(hour // m, 2)

    own_rows = pl.ds(EDGE, rows)
    loads = []
    for z, n in ((0, STEP), (cols - STEP, STEP), (STEP, cols - 2 * STEP)):
        for src, dst in ((s_hbm, es), (p_hbm, ep)):
            lanes = pl.ds(z, n)
            loads.append(pltpu.make_async_copy(src.at[0, :, lanes], dst.at[own_rows, lanes], local.at[len(loads)]))
    loads.append(pltpu.make_async_copy(c_hbm.at[0], ct, local.at[len(loads)]))
    for copy in loads:
        copy.start()

    barrier = pltpu.get_barrier_semaphore()
    lats = [up, down] if n_lat > 2 else [down]
    lons = [left, right] if n_lon > 2 else [right]
    peers = [{"lon": z} for z in lons] + [{"lat": x} for x in lats]
    peers += [{"lat": x, "lon": z} for x in lats for z in lons]
    peers += [{"hour": flip(bit)} for bit in range(bits)]
    for peer in peers:
        pl.semaphore_signal(barrier, inc=1, device_id=peer, device_id_type=MESH)

    sd_l[...] = jnp.zeros_like(sd_l)
    sd_r[...] = jnp.zeros_like(sd_r)
    pl.semaphore_wait(barrier, len(peers))

    sent = []

    def send(src, dst, peer):
        at = len(sent)
        copy = pltpu.make_async_remote_copy(
            src_ref=src, dst_ref=dst, send_sem=sends.at[at], recv_sem=recvs.at[at],
            device_id=peer, device_id_type=MESH,
        )
        copy.start()
        sent.append(copy)
        return copy

    def fill(at, n):
        r, lanes = slice(EDGE + at, EDGE + at + n), slice(at, at + n)
        st_l[0:EDGE, lanes] = es[r, 0:STEP].T[0:EDGE]
        st_r[0:EDGE, lanes] = es[r, cols - STEP : cols].T[STEP - EDGE :]
        st_l[EDGE:, lanes] = ep[r, 0:STEP].T[0:RADIUS]
        st_r[EDGE:, lanes] = ep[r, cols - STEP : cols].T[STEP - RADIUS :]

    early, late = [], []
    for src, dst in ((s_hbm, es), (p_hbm, ep)):
        early.append(send(src.at[0, pl.ds(rows - EDGE, EDGE)], dst.at[pl.ds(0, EDGE), pl.ds(0, cols)], {"lat": down}))
    for copy in loads[:4]:
        copy.wait()
    fill(0, STEP)
    fill(rows - STEP, STEP)
    first_lanes, last_lanes = pl.ds(0, STEP), pl.ds(rows - STEP, STEP)
    sides = ((st_l, h_r, left), (st_r, h_l, right))
    for stage, dst, z in sides:
        early.append(send(stage.at[:, first_lanes], dst.at[:, pl.ds(STEP, STEP)], {"lon": z}))
        early.append(send(stage.at[:, last_lanes], dst.at[:, first_lanes], {"lat": down, "lon": z}))
    fill(STEP, rows - 2 * STEP)
    for stage, dst, z in sides:
        late.append(send(stage.at[:, first_lanes], dst.at[:, pl.ds(STEP + rows, STEP)], {"lat": up, "lon": z}))
        late.append(send(stage.at[:, pl.ds(STEP, rows - STEP)], dst.at[:, pl.ds(2 * STEP, rows - STEP)], {"lon": z}))
    for src, dst in ((s_hbm, es), (p_hbm, ep)):
        late.append(send(src.at[0, pl.ds(0, EDGE)], dst.at[pl.ds(EDGE + rows, EDGE), pl.ds(0, cols)], {"lat": up}))

    top, bottom = slice(0, EDGE), slice(EDGE + rows, tall)

    def beside(at, n, start, skip, size):
        lanes = slice(at, at + n)
        for dst, low, high in ((es, 0, EDGE), (ep, EDGE, EDGE + RADIUS)):
            ones = jnp.ones((STEP - 2 * (high - low), n), F32)
            block = jnp.concatenate([h_r[low:high, lanes], ones, h_l[low:high, lanes]], axis=0).T
            dst[start : start + size, cols:wide] = block[skip : skip + size]

    weight = w_ref[0]
    t_pair[...] = stacked_cols(2 * STEP)
    t_last[...] = stacked_cols(STEP)
    for n, ref in by_height.items():
        ref[...] = stacked_rows(n)
    for copy in loads[4:]:
        copy.wait()
    for copy in early:
        copy.wait_recv()
    beside(0, 2 * STEP, 0, STEP - EDGE, STEP + EDGE)
    es[top, :] = jnp.where(lat > 0, es[top, :], 0.0)

    def rest():
        for copy in late:
            copy.wait_recv()
        beside(2 * STEP, rows, STEP + EDGE, 0, rows - STEP + EDGE)
        es[bottom, :] = jnp.where(lat < n_lat - 1, es[bottom, :], 0.0)

    def lifted(c):
        at, n = pieces[c]
        span = slice(at + RADIUS, at + RADIUS + n + EDGE)
        a = col_pass(t_pair, t_last, row_pass(by_height[n + EDGE], es[at : at + n + 2 * EDGE, :]), wide)
        first[span, :] = a
        u = jnp.exp(PHI * jnp.log(ep[span, :] / a))
        if c == 0 or c == count - 1:
            e = lax.broadcasted_iota(jnp.int32, u.shape, 0) + (at + RADIUS)
            inside = ((lat > 0) | (e >= EDGE)) & ((lat < n_lat - 1) | (e < EDGE + rows))
            u = jnp.where(inside, u, 0.0)
        lift[span, :] = u

    def logs(c):
        at, n = pieces[c]
        b = col_pass(t_pair, t_last, row_pass(by_height[n], lift[at + RADIUS : at + RADIUS + n + EDGE, :]), cols)
        logb = jnp.log(b)
        mine = slice(at, at + n)
        own[0, mine, :] = weight * logb
        own[1, mine, :] = ct[mine, :] * jnp.exp(-PHI * logb)
        scale[mine, :] = PHI / b
        r = pl.ds(at, n)
        return send(own.at[1 - side, r], got.at[r], {"hour": flip(0)})

    def join(c, bit, copy):
        copy.wait_recv()
        at, n = pieces[c]
        mine = slice(at, at + n)
        r = pl.ds(at, n)
        if bit == 0:
            value = own[side, mine, :] + got[mine, :]
        else:
            value = part[bit - 1, mine, :] + other[bit - 1, mine, :]
        if bit == bits - 1:
            both[side, mine, :] = value
            return send(both.at[side, r], both.at[side, r], {"hour": flip(0)})
        part[bit, mine, :] = value
        return send(part.at[bit, r], other.at[bit, r], {"hour": flip(bit + 1)})

    def second(c, copy):
        copy.wait_recv()
        at, n = pieces[c]
        mine = slice(at, at + n)
        d = jnp.exp(PHI * both[0, mine, :]) * (weight * both[1, mine, :] - own[1, mine, :]) * scale[mine, :]
        ds[at + EDGE : at + EDGE + n, 0:cols] = d
        sd_l[c, :, 0:n] = d[:, 0:STEP].T[0:EDGE]
        sd_r[c, :, 0:n] = d[:, cols - STEP : cols].T[STEP - EDGE :]
        main, corner = [], []
        inner = pl.ds(0, cols)
        if c == 0:
            corner.append(send(ds.at[pl.ds(EDGE, EDGE), inner], ds.at[pl.ds(EDGE + rows, EDGE), inner], {"lat": up}))
        if c == count - 1:
            corner.append(send(ds.at[pl.ds(rows, EDGE), inner], ds.at[pl.ds(0, EDGE), inner], {"lat": down}))
        for stage, dst, z in ((sd_l, hd_r, left), (sd_r, hd_l, right)):
            main.append(send(stage.at[c], dst.at[c + 1], {"lon": z}))
            if c == 0:
                corner.append(send(stage.at[c], dst.at[count + 1], {"lat": up, "lon": z}))
            if c == count - 1:
                corner.append(send(stage.at[c], dst.at[0], {"lat": down, "lon": z}))
        return main, corner

    def side_block(i, n):
        zeros = jnp.zeros((STEP - 2 * EDGE, n), F32)
        return jnp.concatenate([hd_r[i, :, 0:n], zeros, hd_l[i, :, 0:n]], axis=0).T

    def take_main(c, copies):
        for copy in copies:
            copy.wait_recv()
        at, n = pieces[c]
        ds[EDGE + at : EDGE + at + n, cols:wide] = side_block(c + 1, n)

    def take_corners(copies):
        for copy in copies:
            copy.wait_recv()
        n = pieces[count - 1][1]
        ds[top, cols:wide] = side_block(0, n)[n - EDGE :]
        ds[bottom, cols:wide] = side_block(count + 1, pieces[0][1])[0:EDGE]
        ds[top, :] = jnp.where(lat > 0, ds[top, :], 0.0)
        ds[bottom, :] = jnp.where(lat < n_lat - 1, ds[bottom, :], 0.0)

    def finish(at, n):
        mine = slice(at, at + n)
        o_p[0, mine, :], o_s[0, mine, :] = backward(at, n, held, by_height)

    moving = {}
    joined = 0
    ahead = 3 if bits == 2 else count
    for i, c in enumerate(order):
        lifted(c)
        if 0 < i <= ahead:
            moving[order[i - 1]] = join(order[i - 1], 0, moving[order[i - 1]])
            joined = i
        moving[c] = logs(c)
        if i == 0:
            rest()
    if joined < ahead:
        for c in order[joined:]:
            moving[c] = join(c, 0, moving[c])
        joined = count
    for bit in range(1, bits - 1):
        for c in order:
            moving[c] = join(c, bit, moving[c])
    areas = regions(rows)
    mains, corners = {}, []
    for i, c in enumerate(order):
        if bits > 1:
            moving[c] = join(c, bits - 1, moving[c])
        if joined < count:
            moving[order[joined]] = join(order[joined], 0, moving[order[joined]])
            joined += 1
        for k in range(max(i - 1, 0), i + 1 if i == count - 1 else i):
            mains[order[k]], corner = second(order[k], moving[order[k]])
            corners += corner
        if i == count - 2:
            take_main(order[0], mains[order[0]])
            take_main(order[1], mains[order[1]])
            take_corners(corners)
            finish(*areas[0])
            finish(*areas[1])
            for k in range(2, i):
                take_main(order[k], mains[order[k]])
                finish(*areas[k])
    take_main(order[-2], mains[order[-2]])
    finish(*areas[-2])
    take_main(order[-1], mains[order[-1]])
    for copy in sent:
        copy.wait_send()


def write_out(area, p_ref, s_ref, ds, first, lift, ep, t_pair, t_last, low, high, p_out, s_out, p_last, s_last, done):
    at, n = area
    rows = p_ref.shape[1]
    copies = []

    def write(src, dst):
        copies.append(pltpu.make_async_copy(src, dst, done.at[len(copies)]))
        copies[-1].start()

    for r in (pl.ds(0, at), pl.ds(at + n, rows - at - n)):
        write(p_ref.at[0, r], p_out.at[0, r])
        write(s_ref.at[0, r], s_out.at[0, r])
    refs = (ds, first, lift, ep, t_pair, t_last)
    p_last[...], s_last[...] = backward(at, n, refs, {n: low, n + EDGE: high})
    write(p_last, p_out.at[0, pl.ds(at, n)])
    write(s_last, s_out.at[0, pl.ds(at, n)])
    for copy in copies:
        copy.wait()


def per_device(n_hour, n_lat, n_lon, precip, scaling, hour_weight, cotangent):
    rows, cols = precip.shape[1:]
    tall, wide, lanes = rows + 2 * EDGE, cols + STEP, rows + 2 * STEP
    bits = n_hour.bit_length() - 1
    pieces, _ = plan(rows)
    count = len(pieces)
    assert n_hour == 1 << bits and bits > 0 and min(n_lat, n_lon) > 1
    assert rows % STEP == 0 and cols % (2 * STEP) == 0 and count > 3
    ext, tile = pltpu.VMEM((tall, wide), F32), pltpu.VMEM((rows, cols), F32)
    pair = pltpu.VMEM((2, rows, cols), F32)
    steps = pltpu.VMEM((max(bits - 1, 1), rows, cols), F32)
    copies = 12 + count * (bits + 3) + 6
    out = jax.ShapeDtypeStruct(precip.shape, F32)
    hbm = pl.BlockSpec(memory_space=pl.ANY)
    vmem = pl.BlockSpec(memory_space=pltpu.VMEM)
    held = pltpu.VMEM(precip.shape, F32)
    stage, halo = pltpu.VMEM((EDGE + RADIUS, rows), F32), pltpu.VMEM((EDGE + RADIUS, lanes), F32)
    piece_stage, piece_halo = pltpu.VMEM((count, EDGE, STEP), F32), pltpu.VMEM((count + 2, EDGE, STEP), F32)
    heads = heights(rows)
    fixed = [(8 * STEP, 2 * STEP), (5 * STEP, STEP)] + [(n, 3 * (n + EDGE)) for n in heads]
    held = [pltpu.VMEM(precip.shape, F32)] * 2 + [ext] * 4 + [pltpu.VMEM(k, BF16) for k in fixed]
    size = 4 * (2 * rows * cols + 4 * tall * wide) + sum(2 * k[0] * (-(-k[1] // STEP) * STEP) for k in fixed)
    spare = (64 * 2**20 - size - 2**19) // 1024 * 1024
    made = pl.pallas_call(
        functools.partial(kernel, (n_hour, n_lat, n_lon, rows, cols)),
        out_shape=tuple(held),
        in_specs=[hbm, hbm, pl.BlockSpec(memory_space=pltpu.SMEM), hbm],
        out_specs=tuple([vmem] * len(held)),
        scratch_shapes=[
            ext, tile, pair, tile, steps, steps, pair, tile,
            stage, stage, halo, halo, piece_stage, piece_stage, piece_halo, piece_halo,
            pltpu.SemaphoreType.DMA((7,)),
            pltpu.SemaphoreType.DMA((copies,)), pltpu.SemaphoreType.DMA((copies,)),
        ],
        compiler_params=pltpu.CompilerParams(
            collective_id=0, has_side_effects=True, vmem_limit_bytes=spare
        ),
    )(precip, scaling, hour_weight, cotangent)
    at, n = regions(rows)[-1]
    bands = dict(zip(heads, made[8:]))
    return pl.pallas_call(
        functools.partial(write_out, (at, n)),
        out_shape=(out, out),
        in_specs=[vmem] * 10,
        out_specs=(hbm, hbm),
        scratch_shapes=[
            pltpu.VMEM((n, cols), F32), pltpu.VMEM((n, cols), F32), pltpu.SemaphoreType.DMA((6,)),
        ],
        compiler_params=pltpu.CompilerParams(vmem_limit_bytes=8 * 2**20),
    )(*made[:8], bands[n], bands[n + EDGE])


def solution(mesh):
    field = P("hour", "lat", "lon")
    sizes = [mesh.shape[a] for a in ("hour", "lat", "lon")]
    return jax.shard_map(
        functools.partial(per_device, *sizes), mesh=mesh,
        in_specs=(field, field, P("hour"), field), out_specs=(field, field), check_vma=False,
    )
```
